512 devices in a mesh: ctx: 128 (over x, z_hi, y, core), tp: 4 (over z_lo).
Axes of the slice: x: 4, y: 4, z: 16 (z_hi: 4, z_lo: 4; z = z_hi * 4 + z_lo), core: 2. Of those that a mesh axis runs over, the one named last changes fastest.
Arguments:
- query: bfloat16 [16384, 4096], P('ctx', 'tp'), may hold values from -6 to 6
- keys: bfloat16 [16384, 4096], P('ctx', 'tp'), may hold values from -6 to 6
- values: bfloat16 [16384, 4096], P('ctx', 'tp'), may hold values from -6 to 6
- residues: float32 [4096, 16], P('tp'), may hold values from -0.01953125 to 0.01953125
- rates: float32 [4096, 16], P('tp'), may hold values from 1.8310548e-05 to 0.05
- skip_gain: float32 [4096], P('tp'), may hold values from -4 to 4
- w_out: bfloat16 [4096, 4096], P('tp', 'ctx'), may hold values from -0.375 to 0.375
Outputs:
- mixed: bfloat16 [16384, 4096], P('ctx', 'tp')
The draws below stay inside these ranges and needn't reach their ends.
All inputs are finite; a program needn't handle non-finite values.
Results may differ from the reference program's by a relative error of at most 0.019.
Values may be sent and summed in bfloat16 or wider, within the bound.
No kernel may reach another device: no remote copies, remote signals or barrier semaphores. Data moves between devices by JAX's collectives and lax.ppermute only.
A program may use at most 64 MiB of HBM per device.

```python
import math
import jax
import jax.numpy as jnp
from jax import lax

D = 4096
ORDER = 16
TOK_DEV = 128
LENGTH = 16384
N_CTX = 128


def strengthened(values, key, source, target, parts, factor):
    owner, partner = [(jnp.arange(values.shape[dim]) // (values.shape[dim] // parts)).reshape([-1 if axis == dim else 1 for axis in range(values.ndim)]) for dim in (source, target)]
    chosen = jax.random.permutation(key, parts)[partner]
    strong = (owner == chosen) | (owner == (partner + parts // 2) % parts)
    return jnp.where(strong, factor * values, values)


def levels(stream_key, shape, pieces, least, top_value):
    def one(dim, shards_of):
        steps = jax.random.uniform(jax.random.fold_in(jax.random.fold_in(stream_key, 6), dim), (shards_of,), jnp.float32, least / len(pieces), top_value / len(pieces))
        return jnp.repeat(jnp.exp(steps), shape[dim] // shards_of).reshape((-1,) + (1,) * (len(shape) - dim - 1))

    level = one(*pieces[0])
    for cut in pieces[1:]:
        level = level * one(*cut)
    return level


def gaussian(rng, dims, scale, limit, shards=(), kind=jnp.bfloat16):
    factor_of = levels(rng, dims, shards, -0.22, 0.18) if shards else 1.0
    values = jax.random.normal(rng, dims, jnp.float32) * scale * factor_of
    return jnp.minimum(jnp.maximum(values, -limit), limit).astype(kind)


def heavy_noise(stream_key, dims, spread, limit, split, heavy, kind=jnp.bfloat16):
    drawn = spread * jax.random.normal(stream_key, dims, jnp.float32)
    if split:
        drawn = drawn * levels(stream_key, dims, split, -0.22, 0.18)
    return jnp.clip(strengthened(drawn, jax.random.fold_in(stream_key, 3), *heavy), -limit, limit).astype(kind)


def setup_inputs(seed: int = 0) -> dict:
    streams_of = jax.random.split(jax.random.key(seed), 8)
    query = gaussian(streams_of[0], (LENGTH, D), 1.0, 6.0, ((0, 128), (1, 4)))
    keys = gaussian(streams_of[1], (LENGTH, D), 1.0, 6.0, ((0, 128), (1, 4)))
    values = gaussian(streams_of[2], (LENGTH, D), 1.0, 6.0, ((0, 128), (1, 4)))
    residues = gaussian(streams_of[3], (D, ORDER), (2 / (ORDER * TOK_DEV * N_CTX) ** 0.5), 0.01953125, ((0, 4),), jnp.float32)
    rates = jnp.clip(jnp.exp(math.log(0.05) - 7.912301 * jax.random.uniform(streams_of[4], (D, ORDER), jnp.float32) ** levels(streams_of[4], (D, ORDER), ((0, 4),), -0.2, 0.2)), 1.831054760259576e-05, 0.05)
    skip_gain = gaussian(streams_of[5], (D,), 1.0, 4.0, ((0, 4),), jnp.float32)
    w_out = heavy_noise(streams_of[6], (D, D), D ** -0.5, 0.375, ((0, 4), (1, 128)), (0, 1, 128, 5.5))
    return {"query": query, "keys": keys, "values": values, "residues": residues, "rates": rates, "skip_gain": skip_gain, "w_out": w_out}


def conv_block(args):
    signal, res, rate = args
    length = signal.shape[0]
    times = jnp.arange(length, dtype=jnp.float32)
    filt = jnp.zeros(signal.shape, jnp.float32)
    for pole in range(res.shape[1]):
        filt = filt + res[None, :, pole] * jnp.exp(-times[:, None] * rate[None, :, pole])
    spec = jnp.fft.rfft(signal, 2 * length, axis=0) * jnp.fft.rfft(filt, 2 * length, axis=0)
    return jnp.fft.irfft(spec, 2 * length, axis=0)[:length].astype(jnp.float32)


def reference(query, keys, values, residues, rates, skip_gain, w_out):
    gated_in = (keys.astype(jnp.float32) * values.astype(jnp.float32)).astype(jnp.bfloat16)
    length = query.shape[0]
    width = query.shape[1]
    block = 64
    blocks = width // block
    signal = gated_in.astype(jnp.float32).reshape(length, blocks, block).transpose(1, 0, 2)
    res = residues.reshape(blocks, block, ORDER)
    rate = rates.reshape(blocks, block, ORDER)
    conv = lax.map(conv_block, (signal, res, rate))
    conv = conv.transpose(1, 0, 2).reshape(length, width).astype(jnp.bfloat16)
    gated = (query.astype(jnp.float32) * (conv.astype(jnp.float32) + skip_gain[None, :] * gated_in.astype(jnp.float32))).astype(jnp.bfloat16)
    return jnp.dot(gated, w_out, preferred_element_type=jnp.float32).astype(jnp.bfloat16)
```

```python
import jax
import jax.numpy as jnp
from jax import lax
from jax.experimental import pallas as pl
from jax.experimental.pallas import tpu as pltpu
from jax.sharding import Mesh, PartitionSpec as P

ORDER = 16
TOK = 128
LANES = 128
GROUPS = 8
CHANS = LANES * GROUPS
F32 = jnp.float32
BF16 = jnp.bfloat16


def spread(src, dst, rows):
    for j in range(GROUPS):
        dst[pl.ds(j, rows, stride=GROUPS), :] = src[:, j * LANES : (j + 1) * LANES]


def state_kernel(keys, values, rates, x_out, s_out, x_tok, a_tok, s_rows):
    spread(jnp.exp(-rates[...]), a_tok, ORDER)
    for t in range(0, TOK, 16):
        for j in range(GROUPS):
            here = (pl.ds(t, 16), pl.ds(j * LANES, LANES))
            x = (keys[here].astype(F32) * values[here].astype(F32)).astype(BF16)
            x_out[here] = x
            x_tok[pl.ds(t * GROUPS + j, 16, stride=GROUPS), :] = x.astype(F32)
    decay = [a_tok[m * 8 : m * 8 + 8, :] for m in range(ORDER)]

    def step(i, state):
        for u in range(8):
            x = x_tok[pl.ds(pl.multiple_of((i * 8 + u) * 8, 8), 8), :]
            state = [a * s + x for a, s in zip(decay, state)]
        return state

    state = lax.fori_loop(0, TOK // 8, step, [jnp.zeros((8, LANES), F32)] * ORDER)
    for m in range(ORDER):
        s_rows[pl.ds(m, GROUPS, stride=ORDER), :] = state[m]
    s_out[...] = s_rows[...].astype(BF16)


def mix_kernel(x, q, prefix, rates, res, skip, w, out, x_tok, y_tok, a_tok, r_tok, p_rows, gated):
    spread(jnp.exp(-rates[...]), a_tok, ORDER)
    spread(res[...], r_tok, ORDER)
    p_rows[...] = prefix[...].astype(F32)
    n = x.shape[0]
    for y in range(n):
        for t in range(0, TOK, 16):
            for j in range(GROUPS):
                x_tok[pl.ds(t * GROUPS + j, 16, stride=GROUPS), :] = x[
                    y, pl.ds(t, 16), pl.ds(j * LANES, LANES)
                ].astype(F32)
        decay = [a_tok[m * 8 : m * 8 + 8, :] for m in range(ORDER)]
        resid = [r_tok[m * 8 : m * 8 + 8, :] for m in range(ORDER)]
        state = [
            p_rows[pl.ds(y * ORDER + m, GROUPS, stride=n * ORDER), :] for m in range(ORDER)
        ]

        def step(i, state):
            for u in range(4):
                at = pl.ds(pl.multiple_of((i * 4 + u) * 8, 8), 8)
                xt = x_tok[at, :]
                state = [a * s + xt for a, s in zip(decay, state)]
                terms = [r * s for r, s in zip(resid, state)]
                while len(terms) > 1:
                    terms = [terms[k] + terms[k + 1] for k in range(0, len(terms), 2)]
                y_tok[at, :] = terms[0]
            return state

        lax.fori_loop(0, TOK // 4, step, state)
        for t in range(0, TOK, 16):
            for j in range(GROUPS):
                here = (y, pl.ds(t, 16), pl.ds(j * LANES, LANES))
                conv = y_tok[pl.ds(t * GROUPS + j, 16, stride=GROUPS), :].astype(BF16)
                total = conv.astype(F32) + skip[j : j + 1, :] * x[here].astype(F32)
                gated[pl.ds(y * TOK + t, 16), pl.ds(j * LANES, LANES)] = (
                    q[here].astype(F32) * total
                ).astype(BF16)

    cols = w.shape[0] // out.shape[1]

    @pl.loop(0, out.shape[1])
    def _(z):
        part = lax.dot_general(
            gated[...],
            w[pl.ds(pl.multiple_of(z * cols, cols), cols), :],
            (((1,), (1,)), ((), ())),
            preferred_element_type=F32,
        ).astype(BF16)
        for y in range(n):
            out[y, z] = part[y * TOK : (y + 1) * TOK]


def sum_kernel(recv, out):
    lane = lax.broadcasted_iota(jnp.int32, (TOK, LANES), 1)
    low = lane < 64

    def total(y, half):
        terms = [recv[y, z, :, half * LANES : (half + 1) * LANES].astype(F32) for z in range(4)]
        return (terms[0] + terms[1]) + (terms[2] + terms[3])

    for pair in range(2):
        for half in range(2):
            even = total(2 * pair, half)
            odd = total(2 * pair + 1, half)
            first = jnp.where(low, even, pltpu.roll(odd, 64, 1))
            second = jnp.where(low, pltpu.roll(even, 64, 1), odd)
            at = 2 * half * 2 + pair
            out[:, at * LANES : (at + 1) * LANES] = first.astype(BF16)
            out[:, (at + 2) * LANES : (at + 3) * LANES] = second.astype(BF16)


def params(mib=40):
    return pltpu.CompilerParams(vmem_limit_bytes=mib * 1024 * 1024)


def gather_copies(block, axis, n):
    copies = jnp.broadcast_to(block[None], (n,) + block.shape)
    return lax.all_to_all(copies, axis, split_axis=0, concat_axis=0, tiled=True)


def per_device(query, keys, values, residues, rates, skip_gain, w_out):
    rate_t = rates.T
    res_t = residues.T
    skip = skip_gain.reshape(GROUPS, LANES)
    w_t = w_out.T
    core = lax.axis_index("core")
    group = lax.axis_index("x") * 4 + lax.axis_index("zh")
    member = lax.axis_index("y") * 2 + core

    with jax.named_scope("states"):
        x, state = pl.pallas_call(
            state_kernel,
            out_shape=[
                jax.ShapeDtypeStruct((TOK, CHANS), BF16),
                jax.ShapeDtypeStruct((GROUPS * ORDER, LANES), BF16),
            ],
            scratch_shapes=[
                pltpu.VMEM((TOK * GROUPS, LANES), F32),
                pltpu.VMEM((ORDER * GROUPS, LANES), F32),
                pltpu.VMEM((ORDER * GROUPS, LANES), F32),
            ],
            compiler_params=params(),
        )(keys, values, rate_t)

    with jax.named_scope("scan_member"):
        mine = lax.all_to_all(
            state.reshape(8, ORDER, LANES), ("y", "core"), split_axis=0, concat_axis=0, tiled=True
        ).astype(F32)
        rate_here = lax.dynamic_slice_in_dim(rate_t, member * LANES, LANES, 1)
        one = jnp.exp(-rate_here * TOK)
        inside = [jnp.zeros((ORDER, LANES), F32)]
        for k in range(8):
            inside.append(one * inside[-1] + mine[k])
        total = inside.pop().astype(BF16)
    with jax.named_scope("scan_group"):
        totals = gather_copies(total, ("x", "zh"), 16).astype(F32)
        before = group - 1 - jnp.arange(16, dtype=jnp.int32)
        weight = jnp.where(
            (before >= 0)[:, None, None],
            jnp.exp(
                -rate_here[None] * (TOK * 8 * jnp.maximum(before, 0)).astype(F32)[:, None, None]
            ),
            0.0,
        )
        ahead = jnp.sum(weight * totals, axis=0)
        ages = jnp.arange(8, dtype=F32)[:, None, None] * TOK
        prefix = jnp.exp(-rate_here[None] * ages) * ahead[None] + jnp.stack(inside)
        prefix = prefix.astype(BF16).reshape(4, 2, ORDER, LANES).transpose(1, 0, 2, 3)
        sent = jnp.broadcast_to(prefix[None], (4, 2, 4, ORDER, LANES)).reshape(8, 4, ORDER, LANES)
        prefix = lax.all_to_all(sent, ("y", "core"), split_axis=0, concat_axis=0, tiled=True)

    with jax.named_scope("weights"):
        w_z = gather_copies(w_t, "zh", 4)
        w_x = gather_copies(w_z, "x", 4).reshape(16, 32, CHANS)
        w_other = lax.ppermute(w_x, "core", [(0, 1), (1, 0)])
        w_all = jnp.where(
            core == 0, jnp.stack([w_x, w_other], axis=1), jnp.stack([w_other, w_x], axis=1)
        ).reshape(4 * 4 * 2 * 32, CHANS)

    with jax.named_scope("inputs"):
        xs = gather_copies(x, "y", 4)
        qs = gather_copies(query, "y", 4)

    with jax.named_scope("mix"):
        partial = pl.pallas_call(
            mix_kernel,
            out_shape=jax.ShapeDtypeStruct((4, 4, TOK, 256), BF16),
            scratch_shapes=[
                pltpu.VMEM((TOK * GROUPS, LANES), F32),
                pltpu.VMEM((TOK * GROUPS, LANES), F32),
                pltpu.VMEM((ORDER * GROUPS, LANES), F32),
                pltpu.VMEM((ORDER * GROUPS, LANES), F32),
                pltpu.VMEM((8 * 4 * ORDER, LANES), F32),
                pltpu.VMEM((4 * TOK, CHANS), BF16),
            ],
            compiler_params=params(),
        )(xs, qs, prefix.reshape(8 * 4 * ORDER, LANES), rate_t, res_t, skip, w_all)

    with jax.named_scope("reduce"):
        recv = lax.all_to_all(
            partial.reshape(16, TOK, 256), ("y", "tp"), split_axis=0, concat_axis=0, tiled=True
        ).reshape(4, 4, TOK, 256)
        return pl.pallas_call(
            sum_kernel,
            out_shape=jax.ShapeDtypeStruct((TOK, CHANS), BF16),
            compiler_params=params(),
        )(recv)


def solution(mesh):
    fine = Mesh(mesh.devices.reshape(4, 4, 4, 2, 4), ("x", "zh", "y", "core", "tp"))
    ctx = ("x", "zh", "y", "core")
    placed = (
        P(ctx, "tp"),
        P(ctx, "tp"),
        P(ctx, "tp"),
        P("tp", None),
        P("tp", None),
        P("tp"),
        P("tp", ctx),
    )
    return jax.shard_map(
        per_device, mesh=fine, in_specs=placed, out_specs=P(ctx, "tp"), check_vma=False
    )
```

```python
import jax
import jax.numpy as jnp
from jax import lax
from jax.experimental import pallas as pl
from jax.experimental.pallas import tpu as pltpu
from jax.sharding import Mesh, PartitionSpec as P

ORDER = 16
TOK = 128
LANES = 128
GROUPS = 8
CHANS = LANES * GROUPS
F32 = jnp.float32
BF16 = jnp.bfloat16


def spread(src, dst, rows):
    for j in range(GROUPS):
        dst[pl.ds(j, rows, stride=GROUPS), :] = src[:, j * LANES : (j + 1) * LANES]


def state_kernel(query, keys_far, values_far, rates, xq_out, s_out, keys, values, x_tok, a_tok, s_rows, sems):
    copies = [
        pltpu.make_async_copy(keys_far, keys, sems.at[0]),
        pltpu.make_async_copy(values_far, values, sems.at[1]),
        pltpu.make_async_copy(query, xq_out.at[1], sems.at[2]),
    ]
    for copy in copies:
        copy.start()
    spread(jnp.exp(-rates[...]), a_tok, ORDER)
    copies[0].wait()
    copies[1].wait()
    for t in range(0, TOK, 16):
        for j in range(GROUPS):
            here = (pl.ds(t, 16), pl.ds(j * LANES, LANES))
            x = (keys[here].astype(F32) * values[here].astype(F32)).astype(BF16)
            xq_out[(0,) + here] = x
            x_tok[pl.ds(t * GROUPS + j, 16, stride=GROUPS), :] = x.astype(F32)
    decay = [a_tok[m * 8 : m * 8 + 8, :] for m in range(ORDER)]

    def step(i, state):
        for u in range(8):
            x = x_tok[pl.ds(pl.multiple_of((i * 8 + u) * 8, 8), 8), :]
            state = [a * s + x for a, s in zip(decay, state)]
        return state

    state = lax.fori_loop(0, TOK // 8, step, [jnp.zeros((8, LANES), F32)] * ORDER)
    for m in range(ORDER):
        s_rows[pl.ds(m, GROUPS, stride=ORDER), :] = state[m]
    s_out[...] = s_rows[...].astype(BF16)
    copies[2].wait()


def member_kernel(member, mine, rates, after, copies, inside):
    del after
    rate = rates[:, pl.ds(pl.multiple_of(member[0] * LANES, LANES), LANES)]
    one = jnp.exp(-rate * TOK)
    total = jnp.zeros((ORDER, LANES), F32)
    for k in range(8):
        inside[k] = total
        total = one * total + mine[k].astype(F32)
    for g in range(16):
        copies[g] = total.astype(BF16)


def group_kernel(member, group, totals, inside, rates, sent):
    rate = rates[:, pl.ds(pl.multiple_of(member[0] * LANES, LANES), LANES)]
    one = jnp.exp(-rate * TOK)
    eight = jnp.exp(-rate * (8 * TOK))
    ahead = jnp.zeros((ORDER, LANES), F32)
    for g in range(16):
        ahead = jnp.where(g < group[0], eight * ahead + totals[g].astype(F32), ahead)
    for k in range(8):
        prefix = (ahead + inside[k]).astype(BF16)
        ahead = one * ahead
        for y in range(4):
            sent[2 * y + k % 2, k // 2] = prefix


def mix_kernel(row, b0, b1, b2, b3, prefix, rates, res, skip, w, out, x_tok, y_tok, a_tok, r_tok, p_rows, gated):
    spread(jnp.exp(-rates[...]), a_tok, ORDER)
    spread(res[...], r_tok, ORDER)
    p_rows[...] = prefix[...].astype(F32)
    blocks = (b0, b1, b2, b3)
    n = len(blocks)
    for s, xq in enumerate(blocks):
        y = lax.rem(row[0] + s, n)
        for t in range(0, TOK, 16):
            for j in range(GROUPS):
                x_tok[pl.ds(t * GROUPS + j, 16, stride=GROUPS), :] = xq[
                    0, pl.ds(t, 16), pl.ds(j * LANES, LANES)
                ].astype(F32)
        decay = [a_tok[m * 8 : m * 8 + 8, :] for m in range(ORDER)]
        resid = [r_tok[m * 8 : m * 8 + 8, :] for m in range(ORDER)]
        state = [
            p_rows[pl.ds(y * ORDER + m, GROUPS, stride=n * ORDER), :] for m in range(ORDER)
        ]

        def step(i, state):
            for u in range(4):
                at = pl.ds(pl.multiple_of((i * 4 + u) * 8, 8), 8)
                xt = x_tok[at, :]
                state = [a * s + xt for a, s in zip(decay, state)]
                terms = [r * s for r, s in zip(resid, state)]
                while len(terms) > 1:
                    terms = [terms[k] + terms[k + 1] for k in range(0, len(terms), 2)]
                y_tok[at, :] = terms[0]
            return state

        lax.fori_loop(0, TOK // 4, step, state)
        for t in range(0, TOK, 16):
            for j in range(GROUPS):
                here = (pl.ds(t, 16), pl.ds(j * LANES, LANES))
                conv = y_tok[pl.ds(t * GROUPS + j, 16, stride=GROUPS), :].astype(BF16)
                x = xq[(0,) + here].astype(F32)
                total = conv.astype(F32) + skip[j : j + 1, :] * x
                gated[pl.ds(s * TOK + t, 16), pl.ds(j * LANES, LANES)] = (
                    xq[(1,) + here].astype(F32) * total
                ).astype(BF16)

    cols = w.shape[0] // out.shape[0]

    @pl.loop(0, out.shape[0])
    def _(z):
        part = lax.dot_general(
            gated[...],
            w[pl.ds(pl.multiple_of(z * cols, cols), cols), :],
            (((1,), (1,)), ((), ())),
            preferred_element_type=F32,
        ).astype(BF16)
        for s in range(n):
            out[z, lax.rem(row[0] + s, n)] = part[s * TOK : (s + 1) * TOK]


def sum_kernel(recv, out):
    for y in range(4):
        terms = [recv[z, y].astype(F32) for z in range(4)]
        out[y] = ((terms[0] + terms[1]) + (terms[2] + terms[3])).astype(BF16)


def order_kernel(recv, out):
    quarter = lax.broadcasted_iota(jnp.int32, (TOK, LANES), 1) // 32
    tiles = {
        (y, c): recv[y, :, c * LANES : (c + 1) * LANES].astype(F32) for y in range(4) for c in range(2)
    }
    for zh in range(4):
        for pair in range(2):
            total = None
            for k in range(4):
                part = tiles[2 * pair + k // 2, k % 2]
                if k != zh:
                    part = pltpu.roll(part, (k - zh) % 4 * 32, 1)
                total = part if total is None else jnp.where(quarter == k, part, total)
            at = zh * 2 + pair
            out[:, at * LANES : (at + 1) * LANES] = total.astype(BF16)


def place_kernel(row, b0, b1, b2, b3, after, out):
    del after
    for s, block in enumerate((b0, b1, b2, b3)):
        out[lax.rem(row[0] + s, 4)] = block[...]


def params(mib=40):
    return pltpu.CompilerParams(vmem_limit_bytes=mib * 1024 * 1024)


def ring_blocks(block, axis):
    return [block] + [
        lax.ppermute(block, axis, [(i, (i - k) % 4) for i in range(4)]) for k in (1, 2, 3)
    ]


SCALAR = pl.BlockSpec(memory_space=pltpu.SMEM)
FAR = pl.BlockSpec(memory_space=pltpu.HBM)
WHOLE = pl.BlockSpec(memory_space=pltpu.VMEM)


def per_device(query, keys, values, residues, rates, skip_gain, w_out):
    rate_t = rates.T
    res_t = residues.T
    skip = skip_gain.reshape(GROUPS, LANES)
    w_t = w_out.T
    group = (lax.axis_index("x") * 4 + lax.axis_index("zh")).reshape(1)
    member = (lax.axis_index("y") * 2 + lax.axis_index("core")).reshape(1)

    y_here = lax.axis_index("y").reshape(1)
    zh_here = lax.axis_index("zh").reshape(1)

    with jax.named_scope("weights_zh"):
        w_blocks = ring_blocks(w_t, "zh")

    with jax.named_scope("states"):
        xq, state = pl.pallas_call(
            state_kernel,
            out_shape=[
                jax.ShapeDtypeStruct((2, TOK, CHANS), BF16),
                jax.ShapeDtypeStruct((GROUPS * ORDER, LANES), BF16),
            ],
            in_specs=[FAR, FAR, FAR, WHOLE],
            scratch_shapes=[
                pltpu.VMEM((TOK, CHANS), BF16),
                pltpu.VMEM((TOK, CHANS), BF16),
                pltpu.VMEM((TOK * GROUPS, LANES), F32),
                pltpu.VMEM((ORDER * GROUPS, LANES), F32),
                pltpu.VMEM((ORDER * GROUPS, LANES), F32),
                pltpu.SemaphoreType.DMA((3,)),
            ],
            compiler_params=params(60),
        )(query, keys, values, rate_t)

    with jax.named_scope("scan_member"):
        mine = lax.all_to_all(
            state.reshape(8, ORDER, LANES), ("y", "core"), split_axis=0, concat_axis=0, tiled=True
        )
    with jax.named_scope("weights_zh"):
        w_z = pl.pallas_call(
            place_kernel,
            in_specs=[SCALAR] + [WHOLE] * 4 + [FAR],
            out_shape=jax.ShapeDtypeStruct((4, 32, CHANS), BF16),
            compiler_params=params(),
        )(zh_here, *w_blocks, mine)
        w_all = lax.all_gather(w_z, ("x", "core"), axis=0, tiled=True).reshape(1024, CHANS)

    with jax.named_scope("scan_member"):
        totals, inside = pl.pallas_call(
            member_kernel,
            in_specs=[SCALAR, WHOLE, WHOLE, FAR],
            out_shape=[
                jax.ShapeDtypeStruct((16, ORDER, LANES), BF16),
                jax.ShapeDtypeStruct((8, ORDER, LANES), F32),
            ],
            compiler_params=params(),
        )(member, mine, rate_t, w_z)
    with jax.named_scope("scan_group"):
        totals = lax.all_to_all(totals, ("x", "zh"), split_axis=0, concat_axis=0, tiled=True)
        sent = pl.pallas_call(
            group_kernel,
            in_specs=[SCALAR, SCALAR, WHOLE, WHOLE, WHOLE],
            out_shape=jax.ShapeDtypeStruct((8, 4, ORDER, LANES), BF16),
            compiler_params=params(),
        )(member, group, totals, inside, rate_t)
        prefix = lax.all_to_all(sent, ("y", "core"), split_axis=0, concat_axis=0, tiled=True)

    with jax.named_scope("inputs"):
        blocks = ring_blocks(xq, "y")

    with jax.named_scope("mix"):
        partial = pl.pallas_call(
            mix_kernel,
            in_specs=[SCALAR] + [WHOLE] * 9,
            out_shape=jax.ShapeDtypeStruct((4, 4, TOK, 256), BF16),
            scratch_shapes=[
                pltpu.VMEM((TOK * GROUPS, LANES), F32),
                pltpu.VMEM((TOK * GROUPS, LANES), F32),
                pltpu.VMEM((ORDER * GROUPS, LANES), F32),
                pltpu.VMEM((ORDER * GROUPS, LANES), F32),
                pltpu.VMEM((8 * 4 * ORDER, LANES), F32),
                pltpu.VMEM((4 * TOK, CHANS), BF16),
            ],
            compiler_params=params(),
        )(y_here, *blocks, prefix.reshape(8 * 4 * ORDER, LANES), rate_t, res_t, skip, w_all)

    with jax.named_scope("reduce"):
        recv = lax.all_to_all(partial, "tp", split_axis=0, concat_axis=0, tiled=True)
        shares = pl.pallas_call(
            sum_kernel,
            out_shape=jax.ShapeDtypeStruct((4, TOK, 256), BF16),
            compiler_params=params(),
        )(recv)
        cols = lax.all_to_all(shares, "y", split_axis=0, concat_axis=0, tiled=True)
        return pl.pallas_call(
            order_kernel,
            out_shape=jax.ShapeDtypeStruct((TOK, CHANS), BF16),
            compiler_params=params(),
        )(cols)


def solution(mesh):
    fine = Mesh(mesh.devices.reshape(4, 4, 4, 2, 4), ("x", "zh", "y", "core", "tp"))
    ctx = ("x", "zh", "y", "core")
    placed = (
        P(ctx, "tp"),
        P(ctx, "tp"),
        P(ctx, "tp"),
        P("tp", None),
        P("tp", None),
        P("tp"),
        P("tp", ctx),
    )
    return jax.shard_map(
        per_device, mesh=fine, in_specs=placed, out_specs=P(ctx, "tp"), check_vma=False
    )
```

```python
import jax
import jax.numpy as jnp
from jax import lax
from jax.experimental import pallas as pl
from jax.experimental.pallas import tpu as pltpu
from jax.sharding import Mesh, PartitionSpec as P

ORDER = 16
TOK = 128
LANES = 128
GROUPS = 8
CHANS = LANES * GROUPS
COLS = 32
W_ROWS = GROUPS * COLS
PACK = W_ROWS + ORDER
F32 = jnp.float32
BF16 = jnp.bfloat16

SCALAR = pl.BlockSpec(memory_space=pltpu.SMEM)
WHOLE = pl.BlockSpec(memory_space=pltpu.VMEM)
FAR = pl.BlockSpec(memory_space=pltpu.HBM)


def params(mib=40):
    return pltpu.CompilerParams(vmem_limit_bytes=mib * 1024 * 1024)


def spread(src, dst, rows):
    for j in range(GROUPS):
        dst[pl.ds(j, rows, stride=GROUPS), :] = src[:, j * LANES : (j + 1) * LANES]


def per_pole(ref):
    return [ref[m * GROUPS : (m + 1) * GROUPS, :] for m in range(ORDER)]


def tree_sum(terms):
    while len(terms) > 1:
        terms = [terms[k] + terms[k + 1] for k in range(0, len(terms), 2)]
    return terms[0]


def token_rows(t):
    return pl.ds(pl.multiple_of(t * GROUPS, GROUPS), GROUPS)


def state_kernel(keys_far, values_far, rates, x_out, tok_out, s_out, keys, values, a_tok, s_rows, sems):
    copies = [
        pltpu.make_async_copy(keys_far, keys, sems.at[0]),
        pltpu.make_async_copy(values_far, values, sems.at[1]),
    ]
    for copy in copies:
        copy.start()
    spread(jnp.exp(-rates[...]), a_tok, ORDER)
    for copy in copies:
        copy.wait()
    for t in range(0, TOK, 16):
        for j in range(GROUPS):
            here = (pl.ds(t, 16), pl.ds(j * LANES, LANES))
            x = (keys[here].astype(F32) * values[here].astype(F32)).astype(BF16)
            x_out[here] = x
            tok_out[pl.ds(t * GROUPS + j, 16, stride=GROUPS), :] = x.astype(F32)
    decay = per_pole(a_tok)

    def step(i, state):
        for u in range(8):
            x = tok_out[token_rows(i * 8 + u), :]
            state = [a * s + x for a, s in zip(decay, state)]
        return state

    state = lax.fori_loop(0, TOK // 8, step, [jnp.zeros((GROUPS, LANES), F32)] * ORDER)
    for m in range(ORDER):
        s_rows[pl.ds(m, GROUPS, stride=ORDER), :] = state[m]
    s_out[...] = s_rows[...].astype(BF16)


def local_kernel(x_tok, rates, res, y_tok, a_tok, r_tok):
    spread(jnp.exp(-rates[...]), a_tok, ORDER)
    spread(res[...], r_tok, ORDER)
    decay = per_pole(a_tok)
    resid = per_pole(r_tok)

    def step(i, state):
        for u in range(4):
            x = x_tok[token_rows(i * 4 + u), :]
            state = [a * s + x for a, s in zip(decay, state)]
            y_tok[token_rows(i * 4 + u), :] = tree_sum([r * s for r, s in zip(resid, state)])
        return state

    lax.fori_loop(0, TOK // 4, step, [jnp.zeros((GROUPS, LANES), F32)] * ORDER)


def member_kernel(member, mine, rates, w_t, packed, inside):
    rate = rates[:, pl.ds(pl.multiple_of(member[0] * LANES, LANES), LANES)]
    one = jnp.exp(-rate * TOK)
    total = jnp.zeros((ORDER, LANES), F32)
    for k in range(8):
        inside[k] = total
        total = one * total + mine[k].astype(F32)
    total = total.astype(BF16)
    for d in range(4):
        for j in range(GROUPS):
            packed[d, j * COLS : (j + 1) * COLS, :] = w_t[:, j * LANES : (j + 1) * LANES]
        packed[d, W_ROWS:, :] = total


def group_kernel(member, group, packs, inside, rates, sent):
    rate = rates[:, pl.ds(pl.multiple_of(member[0] * LANES, LANES), LANES)]
    one = jnp.exp(-rate * TOK)
    eight = jnp.exp(-rate * (8 * TOK))
    ahead = jnp.zeros((ORDER, LANES), F32)
    for g in range(16):
        total = packs[g // 4, g % 4, W_ROWS:, :].astype(F32)
        ahead = jnp.where(g < group[0], eight * ahead + total, ahead)
    for k in range(8):
        sent[k] = (ahead + inside[k]).astype(BF16)
        ahead = one * ahead


def join_kernel(core, own, other, w):
    for half, packs in enumerate((own, other)):
        side = lax.rem(core[0] + half, 2)
        for x in range(4):
            for zh in range(4):
                rows = pl.ds(pl.multiple_of(side * 128 + zh * COLS, COLS), COLS)
                for j in range(GROUPS):
                    w[x, rows, j * LANES : (j + 1) * LANES] = packs[
                        x, zh, j * COLS : (j + 1) * COLS, :
                    ]


def carry_kernel(y_tok, prefix, x, q, rates, res, skip, out, c_tok, a_tok, r_tok, p_rows):
    spread(jnp.exp(-rates[...]), a_tok, ORDER)
    spread(res[...], r_tok, ORDER)
    p_rows[...] = prefix[...].astype(F32)
    decay = per_pole(a_tok)
    state = [
        r * p_rows[pl.ds(m, GROUPS, stride=ORDER), :] for m, r in enumerate(per_pole(r_tok))
    ]

    def step(i, state):
        for u in range(4):
            at = token_rows(i * 4 + u)
            state = [a * s for a, s in zip(decay, state)]
            c_tok[at, :] = y_tok[at, :] + tree_sum(state)
        return state

    lax.fori_loop(0, TOK // 4, step, state)
    for t in range(0, TOK, 16):
        for j in range(GROUPS):
            here = (pl.ds(t, 16), pl.ds(j * LANES, LANES))
            conv = c_tok[pl.ds(t * GROUPS + j, 16, stride=GROUPS), :].astype(BF16)
            total = conv.astype(F32) + skip[j : j + 1, :] * x[here].astype(F32)
            gated = (q[here].astype(F32) * total).astype(BF16)
            for d in range(4):
                out[(d,) + here] = gated


def dot_kernel(gated, w, out):
    @pl.loop(0, 4)
    def _(x):
        rhs = w[x]
        for y in range(4):
            out[x, y] = lax.dot_general(
                gated[y], rhs, (((1,), (1,)), ((), ())), preferred_element_type=F32
            ).astype(BF16)


def sum_kernel(recv, out):
    for y in range(4):
        terms = [recv[z, y].astype(F32) for z in range(4)]
        out[y] = ((terms[0] + terms[1]) + (terms[2] + terms[3])).astype(BF16)


def order_kernel(recv, out):
    quarter = lax.broadcasted_iota(jnp.int32, (TOK, LANES), 1) // 32
    tiles = {
        (y, c): recv[y, :, c * LANES : (c + 1) * LANES].astype(F32)
        for y in range(4)
        for c in range(2)
    }
    for zh in range(4):
        for pair in range(2):
            total = None
            for k in range(4):
                part = tiles[2 * pair + k // 2, k % 2]
                if k != zh:
                    part = pltpu.roll(part, (k - zh) % 4 * 32, 1)
                total = part if total is None else jnp.where(quarter == k, part, total)
            at = zh * 2 + pair
            out[:, at * LANES : (at + 1) * LANES] = total.astype(BF16)


def exchange(blocks, axis):
    return lax.all_to_all(blocks, axis, split_axis=0, concat_axis=0, tiled=True)


def call(kernel, out_shape, scratch=(), specs=None, mib=40):
    extra = {} if specs is None else {"in_specs": specs}
    return pl.pallas_call(
        kernel, out_shape=out_shape, scratch_shapes=list(scratch), compiler_params=params(mib), **extra
    )


def per_device(query, keys, values, residues, rates, skip_gain, w_out):
    rate_t = rates.T
    res_t = residues.T
    skip = skip_gain.reshape(GROUPS, LANES)
    w_t = w_out.T
    group = (lax.axis_index("x") * 4 + lax.axis_index("zh")).reshape(1)
    core = lax.axis_index("core").reshape(1)
    member = lax.axis_index("y").reshape(1) * 2 + core
    poles = pltpu.VMEM((ORDER * GROUPS, LANES), F32)
    by_token = jax.ShapeDtypeStruct((TOK * GROUPS, LANES), F32)

    with jax.named_scope("states"):
        x, x_tok, state = call(
            state_kernel,
            [
                jax.ShapeDtypeStruct((TOK, CHANS), BF16),
                by_token,
                jax.ShapeDtypeStruct((GROUPS * ORDER, LANES), BF16),
            ],
            [
                pltpu.VMEM((TOK, CHANS), BF16),
                pltpu.VMEM((TOK, CHANS), BF16),
                poles,
                poles,
                pltpu.SemaphoreType.DMA((2,)),
            ],
            [FAR, FAR, WHOLE],
            60,
        )(keys, values, rate_t)
    with jax.named_scope("local"):
        y_tok = call(local_kernel, by_token, [poles, poles])(x_tok, rate_t, res_t)
    with jax.named_scope("scan_member"):
        mine = exchange(state.reshape(8, ORDER, LANES), ("y", "core"))
        packed, inside = call(
            member_kernel,
            [
                jax.ShapeDtypeStruct((4, PACK, LANES), BF16),
                jax.ShapeDtypeStruct((8, ORDER, LANES), F32),
            ],
            specs=[SCALAR, WHOLE, WHOLE, WHOLE],
        )(member, mine, rate_t, w_t)
    with jax.named_scope("scan_group"):
        packed = exchange(packed, "zh")
        packed = exchange(jnp.broadcast_to(packed[None], (4, 4, PACK, LANES)), "x")
        sent = call(
            group_kernel,
            jax.ShapeDtypeStruct((8, ORDER, LANES), BF16),
            specs=[SCALAR, SCALAR, WHOLE, WHOLE, WHOLE],
        )(member, group, packed, inside, rate_t)
        prefix = exchange(sent, ("y", "core")).reshape(GROUPS * ORDER, LANES)
    with jax.named_scope("weights"):
        other = lax.ppermute(packed, "core", [(0, 1), (1, 0)])
        w = call(
            join_kernel,
            jax.ShapeDtypeStruct((4, 8 * COLS, CHANS), BF16),
            specs=[SCALAR, WHOLE, WHOLE],
        )(core, packed, other)
    with jax.named_scope("gate"):
        gated = call(
            carry_kernel,
            jax.ShapeDtypeStruct((4, TOK, CHANS), BF16),
            [pltpu.VMEM((TOK * GROUPS, LANES), F32), poles, poles, poles],
        )(y_tok, prefix, x, query, rate_t, res_t, skip)
        gated = exchange(gated, "y")
    with jax.named_scope("project"):
        partial = call(dot_kernel, jax.ShapeDtypeStruct((4, 4, TOK, 256), BF16))(gated, w)
    with jax.named_scope("reduce"):
        shares = call(sum_kernel, jax.ShapeDtypeStruct((4, TOK, 256), BF16))(
            exchange(partial, "tp")
        )
        return call(order_kernel, jax.ShapeDtypeStruct((TOK, CHANS), BF16))(
            exchange(shares, "y")
        )


def solution(mesh):
    fine = Mesh(mesh.devices.reshape(4, 4, 4, 2, 4), ("x", "zh", "y", "core", "tp"))
    ctx = ("x", "zh", "y", "core")
    placed = (
        P(ctx, "tp"),
        P(ctx, "tp"),
        P(ctx, "tp"),
        P("tp", None),
        P("tp", None),
        P("tp"),
        P("tp", ctx),
    )
    return jax.shard_map(
        per_device, mesh=fine, in_specs=placed, out_specs=P(ctx, "tp"), check_vma=False
    )
```

```python
import jax
import jax.numpy as jnp
from jax import lax
from jax.experimental import pallas as pl
from jax.experimental.pallas import tpu as pltpu
from jax.sharding import Mesh, PartitionSpec as P

ORDER = 16
TOK = 128
LANES = 128
GROUPS = 8
CHANS = LANES * GROUPS
COLS = 32
W_ROWS = GROUPS * COLS
PACK = W_ROWS + ORDER
F32 = jnp.float32
BF16 = jnp.bfloat16

SCALAR = pl.BlockSpec(memory_space=pltpu.SMEM)
WHOLE = pl.BlockSpec(memory_space=pltpu.VMEM)
FAR = pl.BlockSpec(memory_space=pltpu.HBM)


def params(mib=40):
    return pltpu.CompilerParams(vmem_limit_bytes=mib * 1024 * 1024)


def tree_sum(terms):
    while len(terms) > 1:
        terms = [terms[k] + terms[k + 1] for k in range(0, len(terms), 2)]
    return terms[0]


def token_rows(t):
    return pl.ds(pl.multiple_of(t * GROUPS, GROUPS), GROUPS)


def prepare_kernel(keys_far, values_far, query_far, out, keys, values, query, sems):
    pairs = ((keys_far, keys), (values_far, values), (query_far, query))
    copies = [pltpu.make_async_copy(a, b, sems.at[i]) for i, (a, b) in enumerate(pairs)]
    for copy in copies:
        copy.start()
    copies[0].wait()
    copies[1].wait()
    for j in range(GROUPS):
        lanes = slice(j * LANES, (j + 1) * LANES)
        out[j, 0] = (keys[:, lanes].astype(F32) * values[:, lanes].astype(F32)).astype(BF16)
    copies[2].wait()
    for j in range(GROUPS):
        out[j, 1] = query[:, j * LANES : (j + 1) * LANES]


def own_channels(member, ref):
    return ref[:, pl.ds(pl.multiple_of(member[0] * LANES, LANES), LANES)]


def per_pole(block):
    return [jnp.broadcast_to(block[m : m + 1], (GROUPS, LANES)) for m in range(ORDER)]


def by_token(blocks, x_tok):
    for k in range(GROUPS):
        x_tok[pl.ds(k, TOK, stride=GROUPS), :] = blocks[k, 0].astype(F32)


def state_kernel(member, blocks, rates, w_far, packed, inside, x_tok, s_rows, w_t, sem):
    copy = pltpu.make_async_copy(w_far, w_t, sem)
    copy.start()
    rate = own_channels(member, rates)
    decay = per_pole(jnp.exp(-rate))
    by_token(blocks, x_tok)

    def step(i, state):
        for u in range(8):
            x = x_tok[token_rows(i * 8 + u), :]
            state = [a * s + x for a, s in zip(decay, state)]
        return state

    state = lax.fori_loop(0, TOK // 8, step, [jnp.zeros((GROUPS, LANES), F32)] * ORDER)
    for m in range(ORDER):
        s_rows[pl.ds(m, GROUPS, stride=ORDER), :] = state[m]
    one = jnp.exp(-rate * TOK)
    total = jnp.zeros((ORDER, LANES), F32)
    for k in range(GROUPS):
        inside[k] = total
        total = one * total + s_rows[k * ORDER : (k + 1) * ORDER, :]
    total = total.astype(BF16)
    copy.wait()
    for d in range(4):
        packed[d, W_ROWS:, :] = total
        for j in range(GROUPS):
            packed[d, j * COLS : (j + 1) * COLS, :] = w_t[:, j * LANES : (j + 1) * LANES]


def local_kernel(member, blocks, rates, res, y_tok, x_tok):
    decay = per_pole(jnp.exp(-own_channels(member, rates)))
    resid = per_pole(own_channels(member, res))
    by_token(blocks, x_tok)

    def step(i, state):
        for u in range(4):
            x = x_tok[token_rows(i * 4 + u), :]
            state = [a * s + x for a, s in zip(decay, state)]
            y_tok[token_rows(i * 4 + u), :] = tree_sum([r * s for r, s in zip(resid, state)])
        return state

    lax.fori_loop(0, TOK // 4, step, [jnp.zeros((GROUPS, LANES), F32)] * ORDER)


def carry_kernel(
    member, group, packs, inside, y_tok, blocks, rates, res, skips, out, c_tok, p_rows
):
    rate = own_channels(member, rates)
    one = jnp.exp(-rate * TOK)
    eight = jnp.exp(-rate * (8 * TOK))
    ahead = jnp.zeros((ORDER, LANES), F32)
    for g in range(16):
        total = packs[g // 4, g % 4].astype(F32)
        ahead = jnp.where(g < group[0], eight * ahead + total, ahead)
    for k in range(GROUPS):
        p_rows[k * ORDER : (k + 1) * ORDER, :] = ahead + inside[k]
        ahead = one * ahead
    decay = per_pole(jnp.exp(-rate))
    resid = per_pole(own_channels(member, res))
    state = [r * p_rows[pl.ds(m, GROUPS, stride=ORDER), :] for m, r in enumerate(resid)]

    def step(i, state):
        for u in range(4):
            at = token_rows(i * 4 + u)
            state = [a * s for a, s in zip(decay, state)]
            c_tok[at, :] = y_tok[at, :] + tree_sum(state)
        return state

    lax.fori_loop(0, TOK // 4, step, state)
    skip = skips[pl.ds(member[0], 1), :]
    for k in range(GROUPS):
        conv = c_tok[pl.ds(k, TOK, stride=GROUPS), :].astype(BF16).astype(F32)
        total = conv + skip * blocks[k, 0].astype(F32)
        gated = (blocks[k, 1].astype(F32) * total).astype(BF16)
        for y in range(4):
            for t0 in range(2):
                out[2 * (2 * y + k % 2) + t0, k // 2] = gated


def copies_kernel(packed, after, out):
    del after
    for d in range(4):
        out[d] = packed[...]


def join_kernel(core, own, other, w):
    first = core[0] == 0
    for x in range(4):
        for j in range(GROUPS):
            rows = slice(j * COLS, (j + 1) * COLS)
            mine = own[x, :, rows, :].reshape(4 * COLS, LANES)
            theirs = other[x, :, rows, :].reshape(4 * COLS, LANES)
            at = slice(x % 2 * CHANS + j * LANES, x % 2 * CHANS + (j + 1) * LANES)
            w[x // 2, at, :LANES] = jnp.where(first, mine, theirs).T
            w[x // 2, at, LANES:] = jnp.where(first, theirs, mine).T


def dot_kernel(gated, w, out, lhs):
    for y in range(4):
        for j in range(GROUPS):
            for t0 in range(2):
                at = t0 * CHANS + j * LANES
                lhs[y * TOK : (y + 1) * TOK, at : at + LANES] = gated[2 * j + t0, y]

    @pl.loop(0, 2)
    def _(t1):
        part = jnp.dot(lhs[...], w[t1], preferred_element_type=F32).astype(BF16)
        for y in range(4):
            out[y, t1] = part[y * TOK : (y + 1) * TOK]


def order_kernel(recv, out):
    quarter = lax.broadcasted_iota(jnp.int32, (TOK, LANES), 1) // 32
    tiles = {
        (y, c): recv[y, 0, :, c * LANES : (c + 1) * LANES].astype(F32)
        + recv[y, 1, :, c * LANES : (c + 1) * LANES].astype(F32)
        for y in range(4)
        for c in range(2)
    }
    for zh in range(4):
        for pair in range(2):
            total = None
            for k in range(4):
                part = tiles[2 * pair + k // 2, k % 2]
                if k != zh:
                    part = pltpu.roll(part, (k - zh) % 4 * 32, 1)
                total = part if total is None else jnp.where(quarter == k, part, total)
            at = zh * 2 + pair
            out[:, at * LANES : (at + 1) * LANES] = total.astype(BF16)


def exchange(blocks, axis):
    return lax.all_to_all(blocks, axis, split_axis=0, concat_axis=0, tiled=True)


def call(kernel, out_shape, scratch=(), specs=None, mib=24):
    extra = {} if specs is None else {"in_specs": specs}
    return pl.pallas_call(
        kernel, out_shape=out_shape, scratch_shapes=list(scratch), compiler_params=params(mib), **extra
    )


def per_device(query, keys, values, residues, rates, skip_gain, w_out):
    rate_t = rates.T
    res_t = residues.T
    skip = skip_gain.reshape(GROUPS, LANES)
    w_t = w_out.T
    group = (lax.axis_index("x") * 4 + lax.axis_index("zh")).reshape(1)
    core = lax.axis_index("core").reshape(1)
    member = lax.axis_index("y").reshape(1) * 2 + core
    tokens = pltpu.VMEM((TOK * GROUPS, LANES), F32)
    rows = pltpu.VMEM((GROUPS * ORDER, LANES), F32)
    members = ("y", "core")

    with jax.named_scope("prepare"):
        half = pltpu.VMEM((TOK, CHANS), BF16)
        blocks = call(
            prepare_kernel,
            jax.ShapeDtypeStruct((GROUPS, 2, TOK, LANES), BF16),
            [half, half, half, pltpu.SemaphoreType.DMA((3,))],
            [FAR] * 3,
            60,
        )(keys, values, query)
        blocks = exchange(blocks, members)
    with jax.named_scope("weights_swap"):
        swap = [(0, 0), (1, 2), (2, 1), (3, 3), (4, 4), (5, 6), (6, 5), (7, 7)]
        w_t = lax.ppermute(w_t, ("x", "t0"), swap)
    with jax.named_scope("states"):
        packed, inside = call(
            state_kernel,
            [
                jax.ShapeDtypeStruct((4, PACK, LANES), BF16),
                jax.ShapeDtypeStruct((GROUPS, ORDER, LANES), F32),
            ],
            [tokens, rows, pltpu.VMEM((COLS, CHANS), BF16), pltpu.SemaphoreType.DMA],
            [SCALAR, WHOLE, WHOLE, FAR],
        )(member, blocks, rate_t, w_t)
        packed = exchange(packed, "zh")
    with jax.named_scope("local"):
        y_tok = call(
            local_kernel,
            jax.ShapeDtypeStruct((TOK * GROUPS, LANES), F32),
            [tokens],
            [SCALAR, WHOLE, WHOLE, WHOLE],
        )(member, blocks, rate_t, res_t)
    with jax.named_scope("scan_x"):
        packed = call(
            copies_kernel,
            jax.ShapeDtypeStruct((4, 4, PACK, LANES), BF16),
            specs=[WHOLE, FAR],
        )(packed, y_tok)
        packed = exchange(packed, "x")
    with jax.named_scope("weights"):
        other = lax.ppermute(packed, "core", [(0, 1), (1, 0)])
        w = call(
            join_kernel,
            jax.ShapeDtypeStruct((2, 2 * CHANS, 8 * COLS), BF16),
            specs=[SCALAR, WHOLE, WHOLE],
        )(core, packed, other)
    with jax.named_scope("gate"):
        gated = call(
            carry_kernel,
            jax.ShapeDtypeStruct((2 * GROUPS, 4, TOK, LANES), BF16),
            [tokens, rows],
            [SCALAR, SCALAR] + [WHOLE] * 7,
        )(member, group, packed[:, :, W_ROWS:], inside, y_tok, blocks, rate_t, res_t, skip)
        gated = exchange(gated, ("y", "core", "t0"))
    with jax.named_scope("project"):
        shares = call(
            dot_kernel,
            jax.ShapeDtypeStruct((4, 2, TOK, 256), BF16),
            [pltpu.VMEM((4 * TOK, 2 * CHANS), BF16)],
        )(gated, w).reshape(8, TOK, 256)
    with jax.named_scope("reduce"):
        shares = exchange(shares, ("y", "t1")).reshape(4, 2, TOK, 256)
        return call(order_kernel, jax.ShapeDtypeStruct((TOK, CHANS), BF16))(shares)


def solution(mesh):
    fine = Mesh(mesh.devices.reshape(4, 4, 4, 2, 2, 2), ("x", "zh", "y", "core", "t1", "t0"))
    ctx = ("x", "zh", "y", "core")
    tp = ("t1", "t0")
    placed = (
        P(ctx, tp),
        P(ctx, tp),
        P(ctx, tp),
        P(tp, None),
        P(tp, None),
        P(tp),
        P(tp, ctx),
    )
    return jax.shard_map(
        per_device, mesh=fine, in_specs=placed, out_specs=P(ctx, tp), check_vma=False
    )
```

```python
import jax
import jax.numpy as jnp
from jax import lax
from jax.experimental import pallas as pl
from jax.experimental.pallas import tpu as pltpu
from jax.sharding import Mesh, PartitionSpec as P

ORDER = 16
TOK = 128
LANES = 128
GROUPS = 8
CHANS = LANES * GROUPS
COLS = 32
W_ROWS = GROUPS * COLS
QUARTER = W_ROWS // 4
PACK = QUARTER + ORDER
F32 = jnp.float32
BF16 = jnp.bfloat16

SCALAR = pl.BlockSpec(memory_space=pltpu.SMEM)
WHOLE = pl.BlockSpec(memory_space=pltpu.VMEM)
FAR = pl.BlockSpec(memory_space=pltpu.HBM)


def params(mib=40):
    return pltpu.CompilerParams(vmem_limit_bytes=mib * 1024 * 1024)


def tree_sum(terms):
    while len(terms) > 1:
        terms = [terms[k] + terms[k + 1] for k in range(0, len(terms), 2)]
    return terms[0]


def token_rows(t):
    return pl.ds(pl.multiple_of(t * GROUPS, GROUPS), GROUPS)


def prepare_kernel(keys_far, values_far, query_far, out, keys, values, query, sems):
    pairs = ((keys_far, keys), (values_far, values), (query_far, query))
    copies = [pltpu.make_async_copy(a, b, sems.at[i]) for i, (a, b) in enumerate(pairs)]
    for copy in copies:
        copy.start()
    copies[0].wait()
    copies[1].wait()
    for j in range(GROUPS):
        lanes = slice(j * LANES, (j + 1) * LANES)
        out[j, 0] = (keys[:, lanes].astype(F32) * values[:, lanes].astype(F32)).astype(BF16)
    copies[2].wait()
    for j in range(GROUPS):
        out[j, 1] = query[:, j * LANES : (j + 1) * LANES]


def own_channels(member, ref):
    return ref[:, pl.ds(pl.multiple_of(member[0] * LANES, LANES), LANES)]


def per_pole(block):
    return [jnp.broadcast_to(block[m : m + 1], (GROUPS, LANES)) for m in range(ORDER)]


def by_token(blocks, x_tok):
    for k in range(GROUPS):
        x_tok[pl.ds(k, TOK, stride=GROUPS), :] = blocks[k, 0].astype(F32)


def state_kernel(member, blocks, rates, w_far, packed, inside, x_tok, s_rows, w_t, sem):
    copy = pltpu.make_async_copy(w_far, w_t, sem)
    copy.start()
    rate = own_channels(member, rates)
    decay = per_pole(jnp.exp(-rate))
    by_token(blocks, x_tok)

    def step(i, state):
        for u in range(8):
            x = x_tok[token_rows(i * 8 + u), :]
            state = [a * s + x for a, s in zip(decay, state)]
        return state

    state = lax.fori_loop(0, TOK // 8, step, [jnp.zeros((GROUPS, LANES), F32)] * ORDER)
    for m in range(ORDER):
        s_rows[pl.ds(m, GROUPS, stride=ORDER), :] = state[m]
    one = jnp.exp(-rate * TOK)
    total = jnp.zeros((ORDER, LANES), F32)
    for k in range(GROUPS):
        inside[k] = total
        total = one * total + s_rows[k * ORDER : (k + 1) * ORDER, :]
    total = total.astype(BF16)
    copy.wait()
    for x in range(4):
        for zh in range(4):
            packed[4 * x + zh, QUARTER:, :] = total
            for half in range(2):
                j = 2 * x + half
                packed[4 * x + zh, half * COLS : (half + 1) * COLS, :] = w_t[
                    :, j * LANES : (j + 1) * LANES
                ]


def local_kernel(member, blocks, rates, res, y_tok, x_tok):
    decay = per_pole(jnp.exp(-own_channels(member, rates)))
    resid = per_pole(own_channels(member, res))
    by_token(blocks, x_tok)

    def step(i, state):
        for u in range(4):
            x = x_tok[token_rows(i * 4 + u), :]
            state = [a * s + x for a, s in zip(decay, state)]
            y_tok[token_rows(i * 4 + u), :] = tree_sum([r * s for r, s in zip(resid, state)])
        return state

    lax.fori_loop(0, TOK // 4, step, [jnp.zeros((GROUPS, LANES), F32)] * ORDER)


def carry_kernel(
    member, group, packs, inside, y_tok, blocks, rates, res, skips, out, c_tok, p_rows
):
    rate = own_channels(member, rates)
    one = jnp.exp(-rate * TOK)
    eight = jnp.exp(-rate * (8 * TOK))
    ahead = jnp.zeros((ORDER, LANES), F32)
    for g in range(16):
        total = packs[g, QUARTER:, :].astype(F32)
        ahead = jnp.where(g < group[0], eight * ahead + total, ahead)
    for k in range(GROUPS):
        p_rows[k * ORDER : (k + 1) * ORDER, :] = ahead + inside[k]
        ahead = one * ahead
    decay = per_pole(jnp.exp(-rate))
    resid = per_pole(own_channels(member, res))
    state = [r * p_rows[pl.ds(m, GROUPS, stride=ORDER), :] for m, r in enumerate(resid)]

    def step(i, state):
        for u in range(4):
            at = token_rows(i * 4 + u)
            state = [a * s for a, s in zip(decay, state)]
            c_tok[at, :] = y_tok[at, :] + tree_sum(state)
        return state

    lax.fori_loop(0, TOK // 4, step, state)
    skip = skips[pl.ds(member[0], 1), :]
    for k in range(GROUPS):
        conv = c_tok[pl.ds(k, TOK, stride=GROUPS), :].astype(BF16).astype(F32)
        total = conv + skip * blocks[k, 0].astype(F32)
        gated = (blocks[k, 1].astype(F32) * total).astype(BF16)
        for y in range(4):
            for t0 in range(2):
                out[2 * (2 * y + k % 2) + t0, k // 2] = gated


def join_kernel(x, core, *refs):
    w = refs[8:]
    first = core[0] == 0
    for k in range(4):
        own, other = refs[k], refs[4 + k]
        start = lax.rem(x[0] + k, 4) * 2 * LANES
        for xs in range(4):
            for half in range(2):
                rows = slice(half * COLS, (half + 1) * COLS)
                mine = own[4 * xs : 4 * xs + 4, rows, :].reshape(4 * COLS, LANES)
                theirs = other[4 * xs : 4 * xs + 4, rows, :].reshape(4 * COLS, LANES)
                at = pl.ds(pl.multiple_of(start + xs % 2 * CHANS + half * LANES, LANES), LANES)
                w[xs // 2][at, :LANES] = jnp.where(first, mine, theirs).T
                w[xs // 2][at, LANES:] = jnp.where(first, theirs, mine).T


def dot_kernel(gated, w0, w1, out, lhs):
    for y in range(4):
        for j in range(GROUPS):
            for t0 in range(2):
                at = t0 * CHANS + j * LANES
                lhs[y * TOK : (y + 1) * TOK, at : at + LANES] = gated[2 * j + t0, y]
    for t1, w in enumerate((w0, w1)):
        part = jnp.dot(lhs[...], w[...], preferred_element_type=F32).astype(BF16)
        for y in range(4):
            out[y, t1] = part[y * TOK : (y + 1) * TOK]


def order_kernel(recv, out):
    quarter = lax.broadcasted_iota(jnp.int32, (TOK, LANES), 1) // 32
    tiles = {
        (y, c): recv[y, 0, :, c * LANES : (c + 1) * LANES].astype(F32)
        + recv[y, 1, :, c * LANES : (c + 1) * LANES].astype(F32)
        for y in range(4)
        for c in range(2)
    }
    for zh in range(4):
        for pair in range(2):
            total = None
            for k in range(4):
                part = tiles[2 * pair + k // 2, k % 2]
                if k != zh:
                    part = pltpu.roll(part, (k - zh) % 4 * 32, 1)
                total = part if total is None else jnp.where(quarter == k, part, total)
            at = zh * 2 + pair
            out[:, at * LANES : (at + 1) * LANES] = total.astype(BF16)


def exchange(blocks, axis):
    return lax.all_to_all(blocks, axis, split_axis=0, concat_axis=0, tiled=True)


def call(kernel, out_shape, scratch=(), specs=None, mib=24):
    extra = {} if specs is None else {"in_specs": specs}
    return pl.pallas_call(
        kernel, out_shape=out_shape, scratch_shapes=list(scratch), compiler_params=params(mib), **extra
    )


def per_device(query, keys, values, residues, rates, skip_gain, w_out):
    rate_t = rates.T
    res_t = residues.T
    skip = skip_gain.reshape(GROUPS, LANES)
    w_t = w_out.T
    group = (lax.axis_index("x") * 4 + lax.axis_index("zh")).reshape(1)
    core = lax.axis_index("core").reshape(1)
    member = lax.axis_index("y").reshape(1) * 2 + core
    tokens = pltpu.VMEM((TOK * GROUPS, LANES), F32)
    rows = pltpu.VMEM((GROUPS * ORDER, LANES), F32)
    members = ("y", "core")

    with jax.named_scope("prepare"):
        half = pltpu.VMEM((TOK, CHANS), BF16)
        blocks = call(
            prepare_kernel,
            jax.ShapeDtypeStruct((GROUPS, 2, TOK, LANES), BF16),
            [half, half, half, pltpu.SemaphoreType.DMA((3,))],
            [FAR] * 3,
            60,
        )(keys, values, query)
        blocks = exchange(blocks, members)
    with jax.named_scope("weights_swap"):
        swap = [(0, 0), (1, 2), (2, 1), (3, 3), (4, 4), (5, 6), (6, 5), (7, 7)]
        w_t = lax.ppermute(w_t, ("x", "t0"), swap)
    with jax.named_scope("states"):
        packed, inside = call(
            state_kernel,
            [
                jax.ShapeDtypeStruct((16, PACK, LANES), BF16),
                jax.ShapeDtypeStruct((GROUPS, ORDER, LANES), F32),
            ],
            [tokens, rows, pltpu.VMEM((COLS, CHANS), BF16), pltpu.SemaphoreType.DMA],
            [SCALAR, WHOLE, WHOLE, FAR],
        )(member, blocks, rate_t, w_t)
        packed = exchange(packed, ("x", "zh"))
    with jax.named_scope("local"):
        y_tok = call(
            local_kernel,
            jax.ShapeDtypeStruct((TOK * GROUPS, LANES), F32),
            [tokens],
            [SCALAR, WHOLE, WHOLE, WHOLE],
        )(member, blocks, rate_t, res_t)
    with jax.named_scope("weights"):
        quarter = packed[:, :QUARTER]
        further = [
            lax.ppermute(quarter, "x", [(i, (i - k) % 4) for i in range(4)]) for k in (1, 2, 3)
        ]
        own = [quarter, *further]
        other = [lax.ppermute(block, "core", [(0, 1), (1, 0)]) for block in own]
        w = call(
            join_kernel,
            [jax.ShapeDtypeStruct((2 * CHANS, 8 * COLS), BF16)] * 2,
            specs=[SCALAR, SCALAR] + [WHOLE] * 8,
        )(lax.axis_index("x").reshape(1), core, *own, *other)
    with jax.named_scope("gate"):
        gated = call(
            carry_kernel,
            jax.ShapeDtypeStruct((2 * GROUPS, 4, TOK, LANES), BF16),
            [tokens, rows],
            [SCALAR, SCALAR] + [WHOLE] * 7,
        )(member, group, packed, inside, y_tok, blocks, rate_t, res_t, skip)
        gated = exchange(gated, ("y", "core", "t0"))
    with jax.named_scope("project"):
        shares = call(
            dot_kernel,
            jax.ShapeDtypeStruct((4, 2, TOK, 256), BF16),
            [pltpu.VMEM((4 * TOK, 2 * CHANS), BF16)],
        )(gated, *w).reshape(8, TOK, 256)
    with jax.named_scope("reduce"):
        shares = exchange(shares, ("y", "t1")).reshape(4, 2, TOK, 256)
        return call(order_kernel, jax.ShapeDtypeStruct((TOK, CHANS), BF16))(shares)


def solution(mesh):
    fine = Mesh(mesh.devices.reshape(4, 4, 4, 2, 2, 2), ("x", "zh", "y", "core", "t1", "t0"))
    ctx = ("x", "zh", "y", "core")
    tp = ("t1", "t0")
    placed = (
        P(ctx, tp),
        P(ctx, tp),
        P(ctx, tp),
        P(tp, None),
        P(tp, None),
        P(tp),
        P(tp, ctx),
    )
    return jax.shard_map(
        per_device, mesh=fine, in_specs=placed, out_specs=P(ctx, tp), check_vma=False
    )
```

```python
import jax
import jax.numpy as jnp
from jax import lax
from jax.experimental import pallas as pl
from jax.experimental.pallas import tpu as pltpu
from jax.sharding import Mesh, PartitionSpec as P

ORDER = 16
TOK = 128
LANES = 128
GROUPS = 8
CHANS = LANES * GROUPS
COLS = 32
F32 = jnp.float32
BF16 = jnp.bfloat16

SCALAR = pl.BlockSpec(memory_space=pltpu.SMEM)
WHOLE = pl.BlockSpec(memory_space=pltpu.VMEM)
FAR = pl.BlockSpec(memory_space=pltpu.HBM)


def params(mib=40):
    return pltpu.CompilerParams(vmem_limit_bytes=mib * 1024 * 1024)


def tree_sum(terms):
    while len(terms) > 1:
        terms = [terms[k] + terms[k + 1] for k in range(0, len(terms), 2)]
    return terms[0]


def token_rows(t):
    return pl.ds(pl.multiple_of(t * GROUPS, GROUPS), GROUPS)


def prepare_kernel(keys_far, values_far, query_far, out, keys, values, query, sems):
    pairs = ((keys_far, keys), (values_far, values), (query_far, query))
    copies = [pltpu.make_async_copy(a, b, sems.at[i]) for i, (a, b) in enumerate(pairs)]
    for copy in copies:
        copy.start()
    copies[0].wait()
    copies[1].wait()
    for j in range(GROUPS):
        lanes = slice(j * LANES, (j + 1) * LANES)
        out[j, 0] = (keys[:, lanes].astype(F32) * values[:, lanes].astype(F32)).astype(BF16)
    copies[2].wait()
    for j in range(GROUPS):
        out[j, 1] = query[:, j * LANES : (j + 1) * LANES]


def own_channels(member, ref):
    return ref[:, pl.ds(pl.multiple_of(member[0] * LANES, LANES), LANES)]


def per_pole(block):
    return [jnp.broadcast_to(block[m : m + 1], (GROUPS, LANES)) for m in range(ORDER)]


def by_token(blocks, x_tok):
    for k in range(GROUPS):
        x_tok[pl.ds(k, TOK, stride=GROUPS), :] = blocks[k, 0].astype(F32)


def state_kernel(member, blocks, rates, after, also, totals, inside, x_tok, s_rows):
    del after, also
    rate = own_channels(member, rates)
    decay = per_pole(jnp.exp(-rate))
    by_token(blocks, x_tok)

    def step(i, state):
        for u in range(8):
            x = x_tok[token_rows(i * 8 + u), :]
            state = [a * s + x for a, s in zip(decay, state)]
        return state

    state = lax.fori_loop(0, TOK // 8, step, [jnp.zeros((GROUPS, LANES), F32)] * ORDER)
    for m in range(ORDER):
        s_rows[pl.ds(m, GROUPS, stride=ORDER), :] = state[m]
    one = jnp.exp(-rate * TOK)
    total = jnp.zeros((ORDER, LANES), F32)
    for k in range(GROUPS):
        inside[k] = total
        total = one * total + s_rows[k * ORDER : (k + 1) * ORDER, :]
    for g in range(16):
        totals[g] = total.astype(BF16)


def local_kernel(member, blocks, rates, res, after, y_tok, x_tok):
    del after
    decay = per_pole(jnp.exp(-own_channels(member, rates)))
    resid = per_pole(own_channels(member, res))
    by_token(blocks, x_tok)

    def step(i, state):
        for u in range(4):
            x = x_tok[token_rows(i * 4 + u), :]
            state = [a * s + x for a, s in zip(decay, state)]
            y_tok[token_rows(i * 4 + u), :] = tree_sum([r * s for r, s in zip(resid, state)])
        return state

    lax.fori_loop(0, TOK // 4, step, [jnp.zeros((GROUPS, LANES), F32)] * ORDER)


def carry_kernel(
    member, group, packs, inside, y_tok, blocks, rates, res, skips, after, out, c_tok, p_rows
):
    del after
    rate = own_channels(member, rates)
    one = jnp.exp(-rate * TOK)
    eight = jnp.exp(-rate * (8 * TOK))
    ahead = jnp.zeros((ORDER, LANES), F32)
    for g in range(16):
        total = packs[g].astype(F32)
        ahead = jnp.where(g < group[0], eight * ahead + total, ahead)
    for k in range(GROUPS):
        p_rows[k * ORDER : (k + 1) * ORDER, :] = ahead + inside[k]
        ahead = one * ahead
    decay = per_pole(jnp.exp(-rate))
    resid = per_pole(own_channels(member, res))
    state = [r * p_rows[pl.ds(m, GROUPS, stride=ORDER), :] for m, r in enumerate(resid)]

    def step(i, state):
        for u in range(4):
            at = token_rows(i * 4 + u)
            state = [a * s for a, s in zip(decay, state)]
            c_tok[at, :] = y_tok[at, :] + tree_sum(state)
        return state

    lax.fori_loop(0, TOK // 4, step, state)
    skip = skips[pl.ds(member[0], 1), :]
    for k in range(GROUPS):
        conv = c_tok[pl.ds(k, TOK, stride=GROUPS), :].astype(BF16).astype(F32)
        total = conv + skip * blocks[k, 0].astype(F32)
        gated = (blocks[k, 1].astype(F32) * total).astype(BF16)
        for y in range(4):
            for t0 in range(2):
                out[2 * (2 * y + k % 2) + t0, k // 2] = gated


def pair_kernel(at, own, other, after, out):
    del after
    low = lax.rem(at[0], 2)
    out[low] = own[...]
    out[1 - low] = other[...]


def quad_kernel(at, own, other, out):
    high = at[0] // 2
    out[high] = own[...]
    out[1 - high] = other[...]


def join_kernel(x, core, *refs):
    first = core[0] == 0
    for k in range(4):
        own, other = refs[k], refs[4 + k]
        xs = lax.rem(x[0] + k, 4)
        for t1 in range(2):

            @pl.when(xs // 2 == t1)
            def _(own=own, other=other, xs=xs, w=refs[8 + t1]):
                for j in range(GROUPS):
                    lanes = slice(j * LANES, (j + 1) * LANES)
                    mine = own[:, :, lanes].reshape(4 * COLS, LANES)
                    theirs = other[:, :, lanes].reshape(4 * COLS, LANES)
                    at = pl.ds(pl.multiple_of(lax.rem(xs, 2) * CHANS + j * LANES, LANES), LANES)
                    w[at, :LANES] = jnp.where(first, mine, theirs).T
                    w[at, LANES:] = jnp.where(first, theirs, mine).T


def dot_kernel(gated, w0, w1, out, lhs):
    for y in range(4):
        for j in range(GROUPS):
            for t0 in range(2):
                at = t0 * CHANS + j * LANES
                lhs[y * TOK : (y + 1) * TOK, at : at + LANES] = gated[2 * j + t0, y]
    for t1, w in enumerate((w0, w1)):
        part = jnp.dot(lhs[...], w[...], preferred_element_type=F32).astype(BF16)
        for y in range(4):
            out[y, t1] = part[y * TOK : (y + 1) * TOK]


def order_kernel(recv, out):
    quarter = lax.broadcasted_iota(jnp.int32, (TOK, LANES), 1) // 32
    tiles = {
        (y, c): recv[y, 0, :, c * LANES : (c + 1) * LANES].astype(F32)
        + recv[y, 1, :, c * LANES : (c + 1) * LANES].astype(F32)
        for y in range(4)
        for c in range(2)
    }
    for zh in range(4):
        for pair in range(2):
            total = None
            for k in range(4):
                part = tiles[2 * pair + k // 2, k % 2]
                if k != zh:
                    part = pltpu.roll(part, (k - zh) % 4 * 32, 1)
                total = part if total is None else jnp.where(quarter == k, part, total)
            at = zh * 2 + pair
            out[:, at * LANES : (at + 1) * LANES] = total.astype(BF16)


def exchange(blocks, axis):
    return lax.all_to_all(blocks, axis, split_axis=0, concat_axis=0, tiled=True)


def call(kernel, out_shape, scratch=(), specs=None, mib=24, flops=0):
    extra = {} if specs is None else {"in_specs": specs}
    if flops:
        extra["cost_estimate"] = pl.CostEstimate(flops=flops, bytes_accessed=0, transcendentals=0)
    return pl.pallas_call(
        kernel, out_shape=out_shape, scratch_shapes=list(scratch), compiler_params=params(mib), **extra
    )


def per_device(query, keys, values, residues, rates, skip_gain, w_out):
    rate_t = rates.T
    res_t = residues.T
    skip = skip_gain.reshape(GROUPS, LANES)
    w_t = w_out.T
    group = (lax.axis_index("x") * 4 + lax.axis_index("zh")).reshape(1)
    core = lax.axis_index("core").reshape(1)
    member = lax.axis_index("y").reshape(1) * 2 + core
    tokens = pltpu.VMEM((TOK * GROUPS, LANES), F32)
    rows = pltpu.VMEM((GROUPS * ORDER, LANES), F32)
    members = ("y", "core")

    with jax.named_scope("prepare"):
        half = pltpu.VMEM((TOK, CHANS), BF16)
        blocks = call(
            prepare_kernel,
            jax.ShapeDtypeStruct((GROUPS, 2, TOK, LANES), BF16),
            [half, half, half, pltpu.SemaphoreType.DMA((3,))],
            [FAR] * 3,
            60,
        )(keys, values, query)
        blocks = exchange(blocks, members)
    with jax.named_scope("weights_zh"):
        zh_here = lax.axis_index("zh").reshape(1)
        w_near = lax.ppermute(w_t, "zh", [(0, 1), (1, 0), (2, 3), (3, 2)])
    with jax.named_scope("weights_pairs"):
        two = call(
            pair_kernel,
            jax.ShapeDtypeStruct((2, COLS, CHANS), BF16),
            specs=[SCALAR, WHOLE, WHOLE, FAR],
            flops=6000000000,
        )(zh_here, w_t, w_near, w_t)
    with jax.named_scope("states"):
        totals, inside = call(
            state_kernel,
            [
                jax.ShapeDtypeStruct((16, ORDER, LANES), BF16),
                jax.ShapeDtypeStruct((GROUPS, ORDER, LANES), F32),
            ],
            [tokens, rows],
            [SCALAR, WHOLE, WHOLE, FAR, FAR],
        )(member, blocks, rate_t, two, w_t)
        packed = exchange(totals, ("x", "zh"))
    with jax.named_scope("weights_quads"):
        ring = [(x, zh, t0) for x in range(4) for zh in range(4) for t0 in range(2)]
        number = {place: i for i, place in enumerate(ring)}

        def swapped(zh_from):
            moves = []
            for x, zh, t0 in ring:
                here = (x, t0) if x % 2 == t0 else (x ^ 1, 1 - t0)
                moves.append((number[here[0], zh_from(zh), here[1]], number[x, zh, t0]))
            return lax.ppermute(two, ("x", "zh", "t0"), moves)

        other_two = swapped(lambda zh: 3 - zh)
        own_two = swapped(lambda zh: zh)
        quarter = call(
            quad_kernel,
            jax.ShapeDtypeStruct((2, 2, COLS, CHANS), BF16),
            specs=[SCALAR, WHOLE, WHOLE],
        )(zh_here, own_two, other_two).reshape(4, COLS, CHANS)
    with jax.named_scope("local"):
        y_tok = call(
            local_kernel,
            jax.ShapeDtypeStruct((TOK * GROUPS, LANES), F32),
            [tokens],
            [SCALAR, WHOLE, WHOLE, WHOLE, FAR],
            flops=2000000000,
        )(member, blocks, rate_t, res_t, quarter)
    with jax.named_scope("weights"):
        further = [
            lax.ppermute(quarter, "x", [(i, (i - k) % 4) for i in range(4)]) for k in (1, 2, 3)
        ]
        own = [quarter, *further]
        other = [lax.ppermute(block, "core", [(0, 1), (1, 0)]) for block in own]
        w = call(
            join_kernel,
            [jax.ShapeDtypeStruct((2 * CHANS, 8 * COLS), BF16)] * 2,
            specs=[SCALAR, SCALAR] + [WHOLE] * 8,
        )(lax.axis_index("x").reshape(1), core, *own, *other)
    with jax.named_scope("gate"):
        gated = call(
            carry_kernel,
            jax.ShapeDtypeStruct((2 * GROUPS, 4, TOK, LANES), BF16),
            [tokens, rows],
            [SCALAR, SCALAR] + [WHOLE] * 7 + [FAR],
        )(member, group, packed, inside, y_tok, blocks, rate_t, res_t, skip, w_t)
        gated = exchange(gated, ("y", "core", "t0"))
    with jax.named_scope("project"):
        shares = call(
            dot_kernel,
            jax.ShapeDtypeStruct((4, 2, TOK, 256), BF16),
            [pltpu.VMEM((4 * TOK, 2 * CHANS), BF16)],
        )(gated, *w).reshape(8, TOK, 256)
    with jax.named_scope("reduce"):
        shares = exchange(shares, ("y", "t1")).reshape(4, 2, TOK, 256)
        return call(order_kernel, jax.ShapeDtypeStruct((TOK, CHANS), BF16))(shares)


def solution(mesh):
    fine = Mesh(mesh.devices.reshape(4, 4, 4, 2, 2, 2), ("x", "zh", "y", "core", "t1", "t0"))
    ctx = ("x", "zh", "y", "core")
    tp = ("t1", "t0")
    placed = (
        P(ctx, tp),
        P(ctx, tp),
        P(ctx, tp),
        P(tp, None),
        P(tp, None),
        P(tp),
        P(tp, ctx),
    )
    return jax.shard_map(
        per_device, mesh=fine, in_specs=placed, out_specs=P(ctx, tp), check_vma=False
    )
```

```python
import jax
import jax.numpy as jnp
from jax import lax
from jax.experimental import pallas as pl
from jax.experimental.pallas import tpu as pltpu
from jax.sharding import Mesh, PartitionSpec as P

ORDER = 16
TOK = 128
LANES = 128
GROUPS = 8
CHANS = LANES * GROUPS
COLS = 32
F32 = jnp.float32
BF16 = jnp.bfloat16

SCALAR = pl.BlockSpec(memory_space=pltpu.SMEM)
WHOLE = pl.BlockSpec(memory_space=pltpu.VMEM)
FAR = pl.BlockSpec(memory_space=pltpu.HBM)


def params(mib=40):
    return pltpu.CompilerParams(vmem_limit_bytes=mib * 1024 * 1024)


def tree_sum(terms):
    while len(terms) > 1:
        terms = [terms[k] + terms[k + 1] for k in range(0, len(terms), 2)]
    return terms[0]


def token_rows(t):
    return pl.ds(pl.multiple_of(t * GROUPS, GROUPS), GROUPS)


def prepare_kernel(keys_far, values_far, query_far, out, keys, values, query, sems):
    pairs = ((keys_far, keys), (values_far, values), (query_far, query))
    copies = [pltpu.make_async_copy(a, b, sems.at[i]) for i, (a, b) in enumerate(pairs)]
    for copy in copies:
        copy.start()
    copies[0].wait()
    copies[1].wait()
    for j in range(GROUPS):
        lanes = slice(j * LANES, (j + 1) * LANES)
        out[j, 0] = (keys[:, lanes].astype(F32) * values[:, lanes].astype(F32)).astype(BF16)
    copies[2].wait()
    for j in range(GROUPS):
        out[j, 1] = query[:, j * LANES : (j + 1) * LANES]


def own_channels(member, ref):
    return ref[:, pl.ds(pl.multiple_of(member[0] * LANES, LANES), LANES)]


def per_pole(block):
    return [jnp.broadcast_to(block[m : m + 1], (GROUPS, LANES)) for m in range(ORDER)]


def by_token(blocks, x_tok):
    for k in range(GROUPS):
        x_tok[pl.ds(k, TOK, stride=GROUPS), :] = blocks[k, 0].astype(F32)


def state_kernel(member, blocks, rates, after, also, totals, inside, x_tok, s_rows):
    del after, also
    rate = own_channels(member, rates)
    decay = per_pole(jnp.exp(-rate))
    by_token(blocks, x_tok)

    def step(i, state):
        for u in range(8):
            x = x_tok[token_rows(i * 8 + u), :]
            state = [a * s + x for a, s in zip(decay, state)]
        return state

    state = lax.fori_loop(0, TOK // 8, step, [jnp.zeros((GROUPS, LANES), F32)] * ORDER)
    for m in range(ORDER):
        s_rows[pl.ds(m, GROUPS, stride=ORDER), :] = state[m]
    one = jnp.exp(-rate * TOK)
    total = jnp.zeros((ORDER, LANES), F32)
    for k in range(GROUPS):
        inside[k] = total
        total = one * total + s_rows[k * ORDER : (k + 1) * ORDER, :]
    for g in range(16):
        totals[g] = total.astype(BF16)


def local_kernel(member, blocks, rates, res, after, y_tok, x_tok):
    del after
    decay = per_pole(jnp.exp(-own_channels(member, rates)))
    resid = per_pole(own_channels(member, res))
    by_token(blocks, x_tok)

    def step(i, state):
        for u in range(4):
            x = x_tok[token_rows(i * 4 + u), :]
            state = [a * s + x for a, s in zip(decay, state)]
            y_tok[token_rows(i * 4 + u), :] = tree_sum([r * s for r, s in zip(resid, state)])
        return state

    lax.fori_loop(0, TOK // 4, step, [jnp.zeros((GROUPS, LANES), F32)] * ORDER)


def carry_kernel(
    member, group, packs, inside, y_tok, blocks, rates, res, skips, after, out, c_tok, p_rows
):
    del after
    rate = own_channels(member, rates)
    one = jnp.exp(-rate * TOK)
    eight = jnp.exp(-rate * (8 * TOK))
    ahead = jnp.zeros((ORDER, LANES), F32)
    for g in range(16):
        total = packs[g].astype(F32)
        ahead = jnp.where(g < group[0], eight * ahead + total, ahead)
    for k in range(GROUPS):
        p_rows[k * ORDER : (k + 1) * ORDER, :] = ahead + inside[k]
        ahead = one * ahead
    decay = per_pole(jnp.exp(-rate))
    resid = per_pole(own_channels(member, res))
    state = [r * p_rows[pl.ds(m, GROUPS, stride=ORDER), :] for m, r in enumerate(resid)]

    def step(i, state):
        for u in range(4):
            at = token_rows(i * 4 + u)
            state = [a * s for a, s in zip(decay, state)]
            c_tok[at, :] = y_tok[at, :] + tree_sum(state)
        return state

    lax.fori_loop(0, TOK // 4, step, state)
    skip = skips[pl.ds(member[0], 1), :]
    for k in range(GROUPS):
        conv = c_tok[pl.ds(k, TOK, stride=GROUPS), :].astype(BF16).astype(F32)
        total = conv + skip * blocks[k, 0].astype(F32)
        gated = (blocks[k, 1].astype(F32) * total).astype(BF16)
        for y in range(4):
            for t0 in range(2):
                out[2 * (2 * y + k % 2) + t0, k // 2] = gated


def pair_kernel(at, own, other, after, out):
    del after
    low = lax.rem(at[0], 2)
    out[low] = own[...]
    out[1 - low] = other[...]


def quad_kernel(at, own, other, after, out):
    del after
    high = at[0] // 2
    out[high] = own[...]
    out[1 - high] = other[...]


def join_kernel(x, core, *refs):
    first = core[0] == 0
    for k in range(4):
        own, other = refs[k], refs[4 + k]
        xs = lax.rem(x[0] + k, 4)
        for t1 in range(2):

            @pl.when(xs // 2 == t1)
            def _(own=own, other=other, xs=xs, w=refs[8 + t1]):
                for j in range(GROUPS):
                    lanes = slice(j * LANES, (j + 1) * LANES)
                    mine = own[:, :, lanes].reshape(4 * COLS, LANES)
                    theirs = other[:, :, lanes].reshape(4 * COLS, LANES)
                    at = pl.ds(pl.multiple_of(lax.rem(xs, 2) * CHANS + j * LANES, LANES), LANES)
                    w[at, :LANES] = jnp.where(first, mine, theirs).T
                    w[at, LANES:] = jnp.where(first, theirs, mine).T


def dot_kernel(gated, w0, w1, out, lhs):
    for y in range(4):
        for j in range(GROUPS):
            for t0 in range(2):
                at = t0 * CHANS + j * LANES
                lhs[y * TOK : (y + 1) * TOK, at : at + LANES] = gated[2 * j + t0, y]
    for t1, w in enumerate((w0, w1)):
        part = jnp.dot(lhs[...], w[...], preferred_element_type=F32).astype(BF16)
        for y in range(4):
            out[y, t1] = part[y * TOK : (y + 1) * TOK]


def order_kernel(recv, out):
    quarter = lax.broadcasted_iota(jnp.int32, (TOK, LANES), 1) // 32
    tiles = {
        (y, c): recv[y, 0, :, c * LANES : (c + 1) * LANES].astype(F32)
        + recv[y, 1, :, c * LANES : (c + 1) * LANES].astype(F32)
        for y in range(4)
        for c in range(2)
    }
    for zh in range(4):
        for pair in range(2):
            total = None
            for k in range(4):
                part = tiles[2 * pair + k // 2, k % 2]
                if k != zh:
                    part = pltpu.roll(part, (k - zh) % 4 * 32, 1)
                total = part if total is None else jnp.where(quarter == k, part, total)
            at = zh * 2 + pair
            out[:, at * LANES : (at + 1) * LANES] = total.astype(BF16)


def exchange(blocks, axis):
    return lax.all_to_all(blocks, axis, split_axis=0, concat_axis=0, tiled=True)


def call(kernel, out_shape, scratch=(), specs=None, mib=24, flops=0):
    extra = {} if specs is None else {"in_specs": specs}
    if flops:
        extra["cost_estimate"] = pl.CostEstimate(flops=flops, bytes_accessed=0, transcendentals=0)
    return pl.pallas_call(
        kernel, out_shape=out_shape, scratch_shapes=list(scratch), compiler_params=params(mib), **extra
    )


def per_device(query, keys, values, residues, rates, skip_gain, w_out):
    rate_t = rates.T
    res_t = residues.T
    skip = skip_gain.reshape(GROUPS, LANES)
    w_t = w_out.T
    group = (lax.axis_index("x") * 4 + lax.axis_index("zh")).reshape(1)
    core = lax.axis_index("core").reshape(1)
    member = lax.axis_index("y").reshape(1) * 2 + core
    tokens = pltpu.VMEM((TOK * GROUPS, LANES), F32)
    rows = pltpu.VMEM((GROUPS * ORDER, LANES), F32)
    members = ("y", "core")

    with jax.named_scope("prepare"):
        half = pltpu.VMEM((TOK, CHANS), BF16)
        blocks = call(
            prepare_kernel,
            jax.ShapeDtypeStruct((GROUPS, 2, TOK, LANES), BF16),
            [half, half, half, pltpu.SemaphoreType.DMA((3,))],
            [FAR] * 3,
            60,
        )(keys, values, query)
        blocks = exchange(blocks, members)
    with jax.named_scope("weights_zh"):
        zh_here = lax.axis_index("zh").reshape(1)
        w_near = lax.ppermute(w_t, "zh", [(0, 1), (1, 0), (2, 3), (3, 2)])
    with jax.named_scope("weights_pairs"):
        two = call(
            pair_kernel,
            jax.ShapeDtypeStruct((2, COLS, CHANS), BF16),
            specs=[SCALAR, WHOLE, WHOLE, FAR],
            flops=6000000000,
        )(zh_here, w_t, w_near, w_t)
    with jax.named_scope("states"):
        totals, inside = call(
            state_kernel,
            [
                jax.ShapeDtypeStruct((16, ORDER, LANES), BF16),
                jax.ShapeDtypeStruct((GROUPS, ORDER, LANES), F32),
            ],
            [tokens, rows],
            [SCALAR, WHOLE, WHOLE, FAR, FAR],
        )(member, blocks, rate_t, two, w_t)
        packed = exchange(totals, ("x", "zh"))
    with jax.named_scope("weights_quads"):
        ring = [(x, zh, t0) for x in range(4) for zh in range(4) for t0 in range(2)]
        number = {place: i for i, place in enumerate(ring)}

        def swapped(zh_from):
            moves = []
            for x, zh, t0 in ring:
                here = (x, t0) if x % 2 == t0 else (x ^ 1, 1 - t0)
                moves.append((number[here[0], zh_from(zh), here[1]], number[x, zh, t0]))
            return lax.ppermute(two, ("x", "zh", "t0"), moves)

        other_two = swapped(lambda zh: 3 - zh)
        own_two = swapped(lambda zh: zh)
    with jax.named_scope("local"):
        y_tok = call(
            local_kernel,
            jax.ShapeDtypeStruct((TOK * GROUPS, LANES), F32),
            [tokens],
            [SCALAR, WHOLE, WHOLE, WHOLE, FAR],
            flops=2000000000,
        )(member, blocks, rate_t, res_t, other_two)
    with jax.named_scope("weights_quads"):
        quarter = call(
            quad_kernel,
            jax.ShapeDtypeStruct((2, 2, COLS, CHANS), BF16),
            specs=[SCALAR, WHOLE, WHOLE, FAR],
        )(zh_here, own_two, other_two, y_tok).reshape(4, COLS, CHANS)
    with jax.named_scope("weights"):
        further = [
            lax.ppermute(quarter, "x", [(i, (i - k) % 4) for i in range(4)]) for k in (1, 2, 3)
        ]
        own = [quarter, *further]
        other = [lax.ppermute(block, "core", [(0, 1), (1, 0)]) for block in own]
        w = call(
            join_kernel,
            [jax.ShapeDtypeStruct((2 * CHANS, 8 * COLS), BF16)] * 2,
            specs=[SCALAR, SCALAR] + [WHOLE] * 8,
        )(lax.axis_index("x").reshape(1), core, *own, *other)
    with jax.named_scope("gate"):
        gated = call(
            carry_kernel,
            jax.ShapeDtypeStruct((2 * GROUPS, 4, TOK, LANES), BF16),
            [tokens, rows],
            [SCALAR, SCALAR] + [WHOLE] * 7 + [FAR],
        )(member, group, packed, inside, y_tok, blocks, rate_t, res_t, skip, quarter)
        gated = exchange(gated, ("y", "core", "t0"))
    with jax.named_scope("project"):
        shares = call(
            dot_kernel,
            jax.ShapeDtypeStruct((4, 2, TOK, 256), BF16),
            [pltpu.VMEM((4 * TOK, 2 * CHANS), BF16)],
        )(gated, *w).reshape(8, TOK, 256)
    with jax.named_scope("reduce"):
        shares = exchange(shares, ("y", "t1")).reshape(4, 2, TOK, 256)
        return call(order_kernel, jax.ShapeDtypeStruct((TOK, CHANS), BF16))(shares)


def solution(mesh):
    fine = Mesh(mesh.devices.reshape(4, 4, 4, 2, 2, 2), ("x", "zh", "y", "core", "t1", "t0"))
    ctx = ("x", "zh", "y", "core")
    tp = ("t1", "t0")
    placed = (
        P(ctx, tp),
        P(ctx, tp),
        P(ctx, tp),
        P(tp, None),
        P(tp, None),
        P(tp),
        P(tp, ctx),
    )
    return jax.shard_map(
        per_device, mesh=fine, in_specs=placed, out_specs=P(ctx, tp), check_vma=False
    )
```

```python
import jax
import jax.numpy as jnp
from jax import lax
from jax.experimental import pallas as pl
from jax.experimental.pallas import tpu as pltpu
from jax.sharding import Mesh, PartitionSpec as P

ORDER = 16
TOK = 128
LANES = 128
GROUPS = 8
CHANS = LANES * GROUPS
COLS = 32
F32 = jnp.float32
BF16 = jnp.bfloat16

SCALAR = pl.BlockSpec(memory_space=pltpu.SMEM)
WHOLE = pl.BlockSpec(memory_space=pltpu.VMEM)
FAR = pl.BlockSpec(memory_space=pltpu.HBM)


def params(mib=40):
    return pltpu.CompilerParams(vmem_limit_bytes=mib * 1024 * 1024)


def tree_sum(terms):
    while len(terms) > 1:
        terms = [terms[k] + terms[k + 1] for k in range(0, len(terms), 2)]
    return terms[0]


def token_rows(t):
    return pl.ds(pl.multiple_of(t * GROUPS, GROUPS), GROUPS)


def prepare_kernel(keys_far, values_far, query_far, out, keys, values, query, sems):
    pairs = ((keys_far, keys), (values_far, values), (query_far, query))
    copies = [pltpu.make_async_copy(a, b, sems.at[i]) for i, (a, b) in enumerate(pairs)]
    for copy in copies:
        copy.start()
    copies[0].wait()
    copies[1].wait()
    for j in range(GROUPS):
        lanes = slice(j * LANES, (j + 1) * LANES)
        out[j, 0] = (keys[:, lanes].astype(F32) * values[:, lanes].astype(F32)).astype(BF16)
    copies[2].wait()
    for j in range(GROUPS):
        out[j, 1] = query[:, j * LANES : (j + 1) * LANES]


def own_channels(member, ref):
    return ref[:, pl.ds(pl.multiple_of(member[0] * LANES, LANES), LANES)]


def per_pole(block):
    return [jnp.broadcast_to(block[m : m + 1], (GROUPS, LANES)) for m in range(ORDER)]


def by_token(blocks, x_tok):
    for k in range(GROUPS):
        x_tok[pl.ds(k, TOK, stride=GROUPS), :] = blocks[k, 0].astype(F32)


def state_kernel(member, blocks, rates, after, also, totals, inside, x_tok, s_rows):
    del after, also
    rate = own_channels(member, rates)
    decay = per_pole(jnp.exp(-rate))
    by_token(blocks, x_tok)

    def step(i, state):
        for u in range(8):
            x = x_tok[token_rows(i * 8 + u), :]
            state = [a * s + x for a, s in zip(decay, state)]
        return state

    state = lax.fori_loop(0, TOK // 8, step, [jnp.zeros((GROUPS, LANES), F32)] * ORDER)
    for m in range(ORDER):
        s_rows[pl.ds(m, GROUPS, stride=ORDER), :] = state[m]
    one = jnp.exp(-rate * TOK)
    total = jnp.zeros((ORDER, LANES), F32)
    for k in range(GROUPS):
        inside[k] = total
        total = one * total + s_rows[k * ORDER : (k + 1) * ORDER, :]
    for g in range(16):
        totals[g] = total.astype(BF16)


def local_kernel(member, blocks, rates, res, after, y_tok, x_tok):
    del after
    decay = per_pole(jnp.exp(-own_channels(member, rates)))
    resid = per_pole(own_channels(member, res))
    by_token(blocks, x_tok)

    def step(i, state):
        for u in range(4):
            x = x_tok[token_rows(i * 4 + u), :]
            state = [a * s + x for a, s in zip(decay, state)]
            y_tok[token_rows(i * 4 + u), :] = tree_sum([r * s for r, s in zip(resid, state)])
        return state

    lax.fori_loop(0, TOK // 4, step, [jnp.zeros((GROUPS, LANES), F32)] * ORDER)


def carry_kernel(
    member, group, packs, inside, y_tok, blocks, rates, res, skips, after, out, c_tok, p_rows
):
    del after
    rate = own_channels(member, rates)
    one = jnp.exp(-rate * TOK)
    eight = jnp.exp(-rate * (8 * TOK))
    ahead = jnp.zeros((ORDER, LANES), F32)
    for g in range(16):
        total = packs[g].astype(F32)
        ahead = jnp.where(g < group[0], eight * ahead + total, ahead)
    for k in range(GROUPS):
        p_rows[k * ORDER : (k + 1) * ORDER, :] = ahead + inside[k]
        ahead = one * ahead
    decay = per_pole(jnp.exp(-rate))
    resid = per_pole(own_channels(member, res))
    state = [r * p_rows[pl.ds(m, GROUPS, stride=ORDER), :] for m, r in enumerate(resid)]

    def step(i, state):
        for u in range(4):
            at = token_rows(i * 4 + u)
            state = [a * s for a, s in zip(decay, state)]
            c_tok[at, :] = y_tok[at, :] + tree_sum(state)
        return state

    lax.fori_loop(0, TOK // 4, step, state)
    skip = skips[pl.ds(member[0], 1), :]
    for k in range(GROUPS):
        conv = c_tok[pl.ds(k, TOK, stride=GROUPS), :].astype(BF16).astype(F32)
        total = conv + skip * blocks[k, 0].astype(F32)
        gated = (blocks[k, 1].astype(F32) * total).astype(BF16)
        for y in range(4):
            for t0 in range(2):
                out[2 * (2 * y + k % 2) + t0, k // 2] = gated


def pair_kernel(at, own, other, after, out):
    del after
    low = lax.rem(at[0], 2)
    out[low] = own[...]
    out[1 - low] = other[...]


def quad_kernel(at, own, other, after, out):
    del after
    high = at[0] // 2
    out[high] = own[...]
    out[1 - high] = other[...]


def join_kernel(x, core, *refs):
    first = core[0] == 0
    for k in range(4):
        own, other = refs[k], refs[4 + k]
        xs = lax.rem(x[0] + k, 4)
        for t1 in range(2):

            @pl.when(xs // 2 == t1)
            def _(own=own, other=other, xs=xs, w=refs[8 + t1]):
                for j in range(GROUPS):
                    lanes = slice(j * LANES, (j + 1) * LANES)
                    mine = own[:, :, lanes].reshape(4 * COLS, LANES)
                    theirs = other[:, :, lanes].reshape(4 * COLS, LANES)
                    at = pl.ds(pl.multiple_of(lax.rem(xs, 2) * CHANS + j * LANES, LANES), LANES)
                    w[at, :LANES] = jnp.where(first, mine, theirs).T
                    w[at, LANES:] = jnp.where(first, theirs, mine).T


def dot_kernel(gated, w0, w1, out, lhs):
    for y in range(4):
        for j in range(GROUPS):
            for t0 in range(2):
                at = t0 * CHANS + j * LANES
                lhs[y * TOK : (y + 1) * TOK, at : at + LANES] = gated[2 * j + t0, y]
    for t1, w in enumerate((w0, w1)):
        part = jnp.dot(lhs[...], w[...], preferred_element_type=F32).astype(BF16)
        for y in range(4):
            out[y, t1] = part[y * TOK : (y + 1) * TOK]


def order_kernel(recv, out):
    quarter = lax.broadcasted_iota(jnp.int32, (TOK, LANES), 1) // 32
    tiles = {
        (y, c): recv[y, 0, :, c * LANES : (c + 1) * LANES].astype(F32)
        + recv[y, 1, :, c * LANES : (c + 1) * LANES].astype(F32)
        for y in range(4)
        for c in range(2)
    }
    for zh in range(4):
        for pair in range(2):
            total = None
            for k in range(4):
                part = tiles[2 * pair + k // 2, k % 2]
                if k != zh:
                    part = pltpu.roll(part, (k - zh) % 4 * 32, 1)
                total = part if total is None else jnp.where(quarter == k, part, total)
            at = zh * 2 + pair
            out[:, at * LANES : (at + 1) * LANES] = total.astype(BF16)


def exchange(blocks, axis):
    return lax.all_to_all(blocks, axis, split_axis=0, concat_axis=0, tiled=True)


def call(kernel, out_shape, scratch=(), specs=None, mib=24, flops=0):
    extra = {} if specs is None else {"in_specs": specs}
    if flops:
        extra["cost_estimate"] = pl.CostEstimate(flops=flops, bytes_accessed=0, transcendentals=0)
    return pl.pallas_call(
        kernel, out_shape=out_shape, scratch_shapes=list(scratch), compiler_params=params(mib), **extra
    )


def per_device(query, keys, values, residues, rates, skip_gain, w_out):
    rate_t = rates.T
    res_t = residues.T
    skip = skip_gain.reshape(GROUPS, LANES)
    w_t = w_out.T
    group = (lax.axis_index("x") * 4 + lax.axis_index("zh")).reshape(1)
    core = lax.axis_index("core").reshape(1)
    member = lax.axis_index("y").reshape(1) * 2 + core
    tokens = pltpu.VMEM((TOK * GROUPS, LANES), F32)
    rows = pltpu.VMEM((GROUPS * ORDER, LANES), F32)
    members = ("y", "core")

    with jax.named_scope("prepare"):
        half = pltpu.VMEM((TOK, CHANS), BF16)
        blocks = call(
            prepare_kernel,
            jax.ShapeDtypeStruct((GROUPS, 2, TOK, LANES), BF16),
            [half, half, half, pltpu.SemaphoreType.DMA((3,))],
            [FAR] * 3,
            60,
        )(keys, values, query)
        blocks = exchange(blocks, members)
    with jax.named_scope("weights_zh"):
        zh_here = lax.axis_index("zh").reshape(1)
        w_near = lax.ppermute(w_t, "zh", [(0, 1), (1, 0), (2, 3), (3, 2)])
    with jax.named_scope("weights_pairs"):
        two = call(
            pair_kernel,
            jax.ShapeDtypeStruct((2, COLS, CHANS), BF16),
            specs=[SCALAR, WHOLE, WHOLE, FAR],
            flops=6000000000,
        )(zh_here, w_t, w_near, w_t)
    with jax.named_scope("states"):
        totals, inside = call(
            state_kernel,
            [
                jax.ShapeDtypeStruct((16, ORDER, LANES), BF16),
                jax.ShapeDtypeStruct((GROUPS, ORDER, LANES), F32),
            ],
            [tokens, rows],
            [SCALAR, WHOLE, WHOLE, FAR, FAR],
        )(member, blocks, rate_t, two, w_t)
        packed = exchange(totals, ("x", "zh"))
    with jax.named_scope("weights_quads"):
        ring = [(x, zh, t0) for x in range(4) for zh in range(4) for t0 in range(2)]
        number = {place: i for i, place in enumerate(ring)}

        def swapped(zh_from):
            moves = []
            for x, zh, t0 in ring:
                here = (x, t0) if x % 2 == t0 else (x ^ 1, 1 - t0)
                moves.append((number[here[0], zh_from(zh), here[1]], number[x, zh, t0]))
            return lax.ppermute(two, ("x", "zh", "t0"), moves)

        other_two = swapped(lambda zh: 3 - zh)
        own_two = swapped(lambda zh: zh)
    with jax.named_scope("local"):
        y_tok = call(
            local_kernel,
            jax.ShapeDtypeStruct((TOK * GROUPS, LANES), F32),
            [tokens],
            [SCALAR, WHOLE, WHOLE, WHOLE, FAR],
            flops=2000000000,
        )(member, blocks, rate_t, res_t, other_two)
    with jax.named_scope("weights_quads"):
        quarter = call(
            quad_kernel,
            jax.ShapeDtypeStruct((2, 2, COLS, CHANS), BF16),
            specs=[SCALAR, WHOLE, WHOLE, FAR],
        )(zh_here, own_two, other_two, y_tok).reshape(4, COLS, CHANS)
    with jax.named_scope("weights"):
        further = [
            lax.ppermute(quarter, "x", [(i, (i - k) % 4) for i in range(4)]) for k in (1, 2, 3)
        ]
        own = [quarter, *further]
        other = [lax.ppermute(block, "core", [(0, 1), (1, 0)]) for block in own]
        w = call(
            join_kernel,
            [jax.ShapeDtypeStruct((2 * CHANS, 8 * COLS), BF16)] * 2,
            specs=[SCALAR, SCALAR] + [WHOLE] * 8,
            flops=79000000000,
        )(lax.axis_index("x").reshape(1), core, *own, *other)
    with jax.named_scope("gate"):
        gated = call(
            carry_kernel,
            jax.ShapeDtypeStruct((2 * GROUPS, 4, TOK, LANES), BF16),
            [tokens, rows],
            [SCALAR, SCALAR] + [WHOLE] * 7 + [FAR],
        )(member, group, packed, inside, y_tok, blocks, rate_t, res_t, skip, quarter)
        gated = exchange(gated, ("y", "core", "t0"))
    with jax.named_scope("project"):
        shares = call(
            dot_kernel,
            jax.ShapeDtypeStruct((4, 2, TOK, 256), BF16),
            [pltpu.VMEM((4 * TOK, 2 * CHANS), BF16)],
        )(gated, *w).reshape(8, TOK, 256)
    with jax.named_scope("reduce"):
        shares = exchange(shares, ("y", "t1")).reshape(4, 2, TOK, 256)
        return call(order_kernel, jax.ShapeDtypeStruct((TOK, CHANS), BF16))(shares)


def solution(mesh):
    fine = Mesh(mesh.devices.reshape(4, 4, 4, 2, 2, 2), ("x", "zh", "y", "core", "t1", "t0"))
    ctx = ("x", "zh", "y", "core")
    tp = ("t1", "t0")
    placed = (
        P(ctx, tp),
        P(ctx, tp),
        P(ctx, tp),
        P(tp, None),
        P(tp, None),
        P(tp),
        P(tp, ctx),
    )
    return jax.shard_map(
        per_device, mesh=fine, in_specs=placed, out_specs=P(ctx, tp), check_vma=False
    )
```

```python
import jax
import jax.numpy as jnp
from jax import lax
from jax.experimental import pallas as pl
from jax.experimental.pallas import tpu as pltpu
from jax.sharding import Mesh, PartitionSpec as P

ORDER = 16
TOK = 128
LANES = 128
GROUPS = 8
CHANS = LANES * GROUPS
COLS = 32
F32 = jnp.float32
BF16 = jnp.bfloat16

SCALAR = pl.BlockSpec(memory_space=pltpu.SMEM)
WHOLE = pl.BlockSpec(memory_space=pltpu.VMEM)
FAR = pl.BlockSpec(memory_space=pltpu.HBM)


def params(mib=40):
    return pltpu.CompilerParams(vmem_limit_bytes=mib * 1024 * 1024)


def tree_sum(terms):
    while len(terms) > 1:
        terms = [terms[k] + terms[k + 1] for k in range(0, len(terms), 2)]
    return terms[0]


def token_rows(t):
    return pl.ds(pl.multiple_of(t * GROUPS, GROUPS), GROUPS)


def prepare_kernel(keys_far, values_far, query_far, out, keys, values, query, sems):
    pairs = ((keys_far, keys), (values_far, values), (query_far, query))
    copies = [pltpu.make_async_copy(a, b, sems.at[i]) for i, (a, b) in enumerate(pairs)]
    for copy in copies:
        copy.start()
    copies[0].wait()
    copies[1].wait()
    for j in range(GROUPS):
        lanes = slice(j * LANES, (j + 1) * LANES)
        out[j, 0] = (keys[:, lanes].astype(F32) * values[:, lanes].astype(F32)).astype(BF16)
    copies[2].wait()
    for j in range(GROUPS):
        out[j, 1] = query[:, j * LANES : (j + 1) * LANES]


def own_channels(member, ref):
    return ref[:, pl.ds(pl.multiple_of(member[0] * LANES, LANES), LANES)]


def per_pole(block):
    return [jnp.broadcast_to(block[m : m + 1], (GROUPS, LANES)) for m in range(ORDER)]


def by_token(blocks, x_tok):
    for k in range(GROUPS):
        x_tok[pl.ds(k, TOK, stride=GROUPS), :] = blocks[k, 0].astype(F32)


def state_kernel(member, blocks, rates, after, also, totals, inside, x_tok, s_rows):
    del after, also
    rate = own_channels(member, rates)
    decay = per_pole(jnp.exp(-rate))
    by_token(blocks, x_tok)

    def step(i, state):
        for u in range(8):
            x = x_tok[token_rows(i * 8 + u), :]
            state = [a * s + x for a, s in zip(decay, state)]
        return state

    state = lax.fori_loop(0, TOK // 8, step, [jnp.zeros((GROUPS, LANES), F32)] * ORDER)
    for m in range(ORDER):
        s_rows[pl.ds(m, GROUPS, stride=ORDER), :] = state[m]
    one = jnp.exp(-rate * TOK)
    total = jnp.zeros((ORDER, LANES), F32)
    for k in range(GROUPS):
        inside[k] = total
        total = one * total + s_rows[k * ORDER : (k + 1) * ORDER, :]
    for g in range(16):
        totals[g] = total.astype(BF16)


def local_kernel(member, blocks, rates, res, after, y_tok, x_tok):
    del after
    decay = per_pole(jnp.exp(-own_channels(member, rates)))
    resid = per_pole(own_channels(member, res))
    by_token(blocks, x_tok)

    def step(i, state):
        for u in range(4):
            x = x_tok[token_rows(i * 4 + u), :]
            state = [a * s + x for a, s in zip(decay, state)]
            y_tok[token_rows(i * 4 + u), :] = tree_sum([r * s for r, s in zip(resid, state)])
        return state

    lax.fori_loop(0, TOK // 4, step, [jnp.zeros((GROUPS, LANES), F32)] * ORDER)


def carry_kernel(
    member, group, packs, inside, y_tok, blocks, rates, res, skips, after, out, c_tok, p_rows
):
    del after
    rate = own_channels(member, rates)
    one = jnp.exp(-rate * TOK)
    eight = jnp.exp(-rate * (8 * TOK))
    ahead = jnp.zeros((ORDER, LANES), F32)
    for g in range(16):
        total = packs[g].astype(F32)
        ahead = jnp.where(g < group[0], eight * ahead + total, ahead)
    for k in range(GROUPS):
        p_rows[k * ORDER : (k + 1) * ORDER, :] = ahead + inside[k]
        ahead = one * ahead
    decay = per_pole(jnp.exp(-rate))
    resid = per_pole(own_channels(member, res))
    state = [r * p_rows[pl.ds(m, GROUPS, stride=ORDER), :] for m, r in enumerate(resid)]

    def step(i, state):
        for u in range(4):
            at = token_rows(i * 4 + u)
            state = [a * s for a, s in zip(decay, state)]
            c_tok[at, :] = y_tok[at, :] + tree_sum(state)
        return state

    lax.fori_loop(0, TOK // 4, step, state)
    skip = skips[pl.ds(member[0], 1), :]
    for k in range(GROUPS):
        conv = c_tok[pl.ds(k, TOK, stride=GROUPS), :].astype(BF16).astype(F32)
        total = conv + skip * blocks[k, 0].astype(F32)
        gated = (blocks[k, 1].astype(F32) * total).astype(BF16)
        for y in range(4):
            for t0 in range(2):
                out[2 * (2 * y + k % 2) + t0, k // 2] = gated


def pair_kernel(at, own, other, after, out):
    del after
    low = lax.rem(at[0], 2)
    out[low] = own[...]
    out[1 - low] = other[...]


def quad_kernel(at, own, other, after, out):
    del after
    high = at[0] // 2
    out[high] = own[...]
    out[1 - high] = other[...]


def join_kernel(x, core, *refs):
    first = core[0] == 0
    for k in range(4):
        own, other = refs[k], refs[4 + k]
        xs = lax.rem(x[0] + k, 4)
        for t1 in range(2):

            @pl.when(xs // 2 == t1)
            def _(own=own, other=other, xs=xs, w=refs[8 + t1]):
                for j in range(GROUPS):
                    lanes = slice(j * LANES, (j + 1) * LANES)
                    mine = own[:, :, lanes].reshape(4 * COLS, LANES)
                    theirs = other[:, :, lanes].reshape(4 * COLS, LANES)
                    at = pl.ds(pl.multiple_of(lax.rem(xs, 2) * CHANS + j * LANES, LANES), LANES)
                    w[at, :LANES] = jnp.where(first, mine, theirs).T
                    w[at, LANES:] = jnp.where(first, theirs, mine).T


def dot_kernel(gated, w0, w1, out, lhs):
    for y in range(4):
        for j in range(GROUPS):
            for t0 in range(2):
                at = t0 * CHANS + j * LANES
                lhs[y * TOK : (y + 1) * TOK, at : at + LANES] = gated[2 * j + t0, y]
    for t1, w in enumerate((w0, w1)):
        part = jnp.dot(lhs[...], w[...], preferred_element_type=F32).astype(BF16)
        for y in range(4):
            out[y, t1] = part[y * TOK : (y + 1) * TOK]


def order_kernel(recv, out):
    quarter = lax.broadcasted_iota(jnp.int32, (TOK, LANES), 1) // 32
    tiles = {
        (y, c): recv[y, 0, :, c * LANES : (c + 1) * LANES].astype(F32)
        + recv[y, 1, :, c * LANES : (c + 1) * LANES].astype(F32)
        for y in range(4)
        for c in range(2)
    }
    for zh in range(4):
        for pair in range(2):
            total = None
            for k in range(4):
                part = tiles[2 * pair + k // 2, k % 2]
                if k != zh:
                    part = pltpu.roll(part, (k - zh) % 4 * 32, 1)
                total = part if total is None else jnp.where(quarter == k, part, total)
            at = zh * 2 + pair
            out[:, at * LANES : (at + 1) * LANES] = total.astype(BF16)


def exchange(blocks, axis):
    return lax.all_to_all(blocks, axis, split_axis=0, concat_axis=0, tiled=True)


def call(kernel, out_shape, scratch=(), specs=None, mib=24, flops=0):
    extra = {} if specs is None else {"in_specs": specs}
    if flops:
        extra["cost_estimate"] = pl.CostEstimate(flops=flops, bytes_accessed=0, transcendentals=0)
    return pl.pallas_call(
        kernel, out_shape=out_shape, scratch_shapes=list(scratch), compiler_params=params(mib), **extra
    )


def per_device(query, keys, values, residues, rates, skip_gain, w_out):
    rate_t = rates.T
    res_t = residues.T
    skip = skip_gain.reshape(GROUPS, LANES)
    w_t = w_out.T
    group = (lax.axis_index("x") * 4 + lax.axis_index("zh")).reshape(1)
    core = lax.axis_index("core").reshape(1)
    member = lax.axis_index("y").reshape(1) * 2 + core
    tokens = pltpu.VMEM((TOK * GROUPS, LANES), F32)
    rows = pltpu.VMEM((GROUPS * ORDER, LANES), F32)
    members = ("y", "core")

    with jax.named_scope("prepare"):
        half = pltpu.VMEM((TOK, CHANS), BF16)
        blocks = call(
            prepare_kernel,
            jax.ShapeDtypeStruct((GROUPS, 2, TOK, LANES), BF16),
            [half, half, half, pltpu.SemaphoreType.DMA((3,))],
            [FAR] * 3,
            60,
        )(keys, values, query)
        blocks = exchange(blocks, members)
    with jax.named_scope("weights_zh"):
        zh_here = lax.axis_index("zh").reshape(1)
        w_near = lax.ppermute(w_t, "zh", [(0, 1), (1, 0), (2, 3), (3, 2)])
    with jax.named_scope("weights_pairs"):
        two = call(
            pair_kernel,
            jax.ShapeDtypeStruct((2, COLS, CHANS), BF16),
            specs=[SCALAR, WHOLE, WHOLE, FAR],
            flops=6000000000,
        )(zh_here, w_t, w_near, w_t)
    with jax.named_scope("states"):
        totals, inside = call(
            state_kernel,
            [
                jax.ShapeDtypeStruct((16, ORDER, LANES), BF16),
                jax.ShapeDtypeStruct((GROUPS, ORDER, LANES), F32),
            ],
            [tokens, rows],
            [SCALAR, WHOLE, WHOLE, FAR, FAR],
        )(member, blocks, rate_t, two, w_t)
        packed = exchange(totals, ("x", "zh"))
    with jax.named_scope("weights_quads"):
        ring = [(x, zh, t0) for x in range(4) for zh in range(4) for t0 in range(2)]
        number = {place: i for i, place in enumerate(ring)}

        def swapped(zh_from):
            moves = []
            for x, zh, t0 in ring:
                here = (x, t0) if x % 2 == t0 else (x ^ 1, 1 - t0)
                moves.append((number[here[0], zh_from(zh), here[1]], number[x, zh, t0]))
            return lax.ppermute(two, ("x", "zh", "t0"), moves)

        other_two = swapped(lambda zh: 3 - zh)
        own_two = swapped(lambda zh: zh)
    with jax.named_scope("local"):
        y_tok = call(
            local_kernel,
            jax.ShapeDtypeStruct((TOK * GROUPS, LANES), F32),
            [tokens],
            [SCALAR, WHOLE, WHOLE, WHOLE, FAR],
            flops=2000000000,
        )(member, blocks, rate_t, res_t, other_two)
    with jax.named_scope("weights_quads"):
        quarter = call(
            quad_kernel,
            jax.ShapeDtypeStruct((2, 2, COLS, CHANS), BF16),
            specs=[SCALAR, WHOLE, WHOLE, FAR],
        )(zh_here, own_two, other_two, y_tok).reshape(4, COLS, CHANS)
    with jax.named_scope("weights"):
        further = [
            lax.ppermute(quarter, "x", [(i, (i - k) % 4) for i in range(4)]) for k in (1, 2, 3)
        ]
        own = [quarter, *further]
        other = [lax.ppermute(block, "core", [(0, 1), (1, 0)]) for block in own]
        w = call(
            join_kernel,
            [jax.ShapeDtypeStruct((2 * CHANS, 8 * COLS), BF16)] * 2,
            specs=[SCALAR, SCALAR] + [WHOLE] * 8,
        )(lax.axis_index("x").reshape(1), core, *own, *other)
    with jax.named_scope("gate"):
        gated = call(
            carry_kernel,
            jax.ShapeDtypeStruct((2 * GROUPS, 4, TOK, LANES), BF16),
            [tokens, rows],
            [SCALAR, SCALAR] + [WHOLE] * 7 + [FAR],
        )(member, group, packed, inside, y_tok, blocks, rate_t, res_t, skip, quarter)
        gated = exchange(gated, ("y", "core", "t0"))
    with jax.named_scope("project"):
        shares = call(
            dot_kernel,
            jax.ShapeDtypeStruct((4, 2, TOK, 256), BF16),
            [pltpu.VMEM((4 * TOK, 2 * CHANS), BF16)],
            mib=50,
        )(gated, *w).reshape(8, TOK, 256)
    with jax.named_scope("reduce"):
        shares = exchange(shares, ("y", "t1")).reshape(4, 2, TOK, 256)
        return call(order_kernel, jax.ShapeDtypeStruct((TOK, CHANS), BF16))(shares)


def solution(mesh):
    fine = Mesh(mesh.devices.reshape(4, 4, 4, 2, 2, 2), ("x", "zh", "y", "core", "t1", "t0"))
    ctx = ("x", "zh", "y", "core")
    tp = ("t1", "t0")
    placed = (
        P(ctx, tp),
        P(ctx, tp),
        P(ctx, tp),
        P(tp, None),
        P(tp, None),
        P(tp),
        P(tp, ctx),
    )
    return jax.shard_map(
        per_device, mesh=fine, in_specs=placed, out_specs=P(ctx, tp), check_vma=False
    )
```
